128 devices in a mesh: tx: 16 (over z, y), dz: 8 (over x, core).
Axes of the slice: x: 4, y: 4, z: 4, core: 2. Of those that a mesh axis runs over, the one named last changes fastest.
Arguments:
- fuel: float32 [256, 2048, 256], P('tx', 'dz'), may hold values from 0 to 1
- heat: float32 [256, 2048, 256], P('tx', 'dz'), may hold values from 0 to 3
- rate: float32 [256, 2048, 256], P('tx', 'dz'), may hold values from 0.02 to 0.2
Outputs:
- image: float32 [4, 256, 256], P(None, 'tx', 'dz')
- fuel_out: float32 [256, 2048, 256], P('tx', 'dz')
- heat_out: float32 [256, 2048, 256], P('tx', 'dz')
The draws below stay inside these ranges and needn't reach their ends.
All inputs are finite; a program needn't handle non-finite values.
Results may differ from the reference program's by a relative error of at most 0.000092.
Values sent between devices are 32-bit elements; how exact they have to be, the bound alone decides.
A program may use at most 128 MiB of HBM per device.

```python
import math
import jax
import jax.numpy as jnp

NY = 256
STEPS = 4
NX = 256
NZ = 2048


def level_of(own_key, dims, pieces, least, largest):
    def one(axis_at, shards_of):
        heights = jax.random.uniform(jax.random.fold_in(jax.random.fold_in(own_key, 6), axis_at), (shards_of,), jnp.float32, least / len(pieces), largest / len(pieces))
        return jnp.repeat(jnp.exp(heights), dims[axis_at] // shards_of).reshape((-1,) + (1,) * (len(dims) - axis_at - 1))

    gain = one(*pieces[0])
    for cut in pieces[1:]:
        gain = gain * one(*cut)
    return gain


def setup_inputs(seed: int = 0) -> dict:
    splits = jax.random.split(jax.random.key(seed), 4)
    return {
        "fuel": jnp.clip(1.0 * jax.random.uniform(splits[0], (NX, NZ, NY), jnp.float32) ** level_of(splits[0], (NX, NZ, NY), ((0, 16), (1, 8)), -0.2, 0.2), 0.0, 1.0),
        "heat": jnp.clip(3.0 * jax.random.uniform(splits[1], (NX, NZ, NY), jnp.float32) ** level_of(splits[1], (NX, NZ, NY), ((0, 16), (1, 8)), -0.2, 0.2), 0.0, 3.0),
        "rate": jnp.clip(jnp.exp(math.log(0.2) - 2.3025851 * jax.random.uniform(splits[2], (NX, NZ, NY), jnp.float32) ** level_of(splits[2], (NX, NZ, NY), ((0, 16), (1, 8)), -0.2, 0.2)), 0.02, 0.2),
    }


FUEL_SPREAD = 0.15
HEAT_SPREAD = 0.12
ACTIVATION = 1.5
RELEASE = 2.0
OPACITY = 1.5


def advance(padded, rate):
    center = padded[:, 1:-1, 1:-1, :]
    across = jnp.pad(center, ((0, 0), (0, 0), (0, 0), (1, 1)))
    beside = padded[:, 2:, 1:-1, :] + padded[:, :-2, 1:-1, :]
    beside = beside + padded[:, 1:-1, 2:, :] + padded[:, 1:-1, :-2, :]
    beside = beside + across[..., 2:] + across[..., :-2]
    fuel_mixed = center[0] + FUEL_SPREAD * (beside[0] - 6.0 * center[0])
    heat_mixed = center[1] + HEAT_SPREAD * (beside[1] - 6.0 * center[1])
    burned = rate * fuel_mixed * jnp.exp(ACTIVATION * heat_mixed / (1.0 + heat_mixed))
    return jnp.stack([fuel_mixed - burned, heat_mixed + RELEASE * burned])


def march(fields, ahead, total_depth):
    fuel_sample = 0.5 * (fields[0] + ahead[0])
    heat_sample = 0.5 * (fields[1] + ahead[1])
    depth = (OPACITY / total_depth) * heat_sample
    before = jnp.cumsum(depth, axis=1) - depth
    weight = jnp.exp(-before) * (1.0 - jnp.exp(-depth))
    glow = heat_sample / (1.0 + heat_sample)
    red = jnp.sum(weight * glow, axis=1)
    green = jnp.sum(weight * fuel_sample, axis=1)
    blue = jnp.sum(weight * fuel_sample * glow, axis=1)
    return jnp.stack([red, green, blue]), jnp.sum(depth, axis=1)[None]


def reference(fuel, heat, rate):
    fields = jnp.stack([fuel, heat])
    for repeat in range(STEPS):
        padded = jnp.pad(fields, ((0, 0), (1, 1), (1, 1), (0, 0)))
        fields = advance(padded, rate)
    ahead = jnp.concatenate([fields[:, :, 1:, :], jnp.zeros_like(fields[:, :, :1, :])], axis=2)
    color, optical = march(fields, ahead, NZ)
    image = jnp.concatenate([color, 1.0 - jnp.exp(-optical)], axis=0)
    return image, fields[0], fields[1]
```

```python
import functools

import jax
import jax.numpy as jnp
from jax import lax
from jax.experimental import pallas as pl
from jax.experimental.pallas import tpu as pltpu
from jax.sharding import PartitionSpec as P

STEPS = 4
FUEL_SPREAD = 0.15
HEAT_SPREAD = 0.12
ACTIVATION = 1.5
RELEASE = 2.0
OPACITY = 1.5
LOG2E = 1.4426950408889634
MESH = pl.DeviceIdType.MESH

PAD = 8
CHUNKS = 4
SEGMENTS = 8


def neighbours_along_lanes(halves, lane):
    first, last = lane == 0, lane == 127
    low, high = halves
    zero = jnp.zeros_like(low)
    up_low, up_high = pltpu.roll(low, 1, 1), pltpu.roll(high, 1, 1)
    down_low, down_high = pltpu.roll(low, 127, 1), pltpu.roll(high, 127, 1)
    return (
        jnp.where(first, zero, up_low) + jnp.where(last, down_high, down_low),
        jnp.where(first, up_low, up_high) + jnp.where(last, zero, down_high),
    )


def split(value):
    high = value.astype(jnp.bfloat16)
    low = (value - high.astype(jnp.float32)).astype(jnp.bfloat16)
    return high, low


def advance(src, dst, rate, adjacent, x, start, rows, matrix):
    center = [[src[f, s, x, pl.ds(start + PAD, rows), :] for s in range(2)] for f in range(2)]
    if matrix:
        parts = [split(jnp.concatenate(center[f], axis=1)) for f in range(2)]
        sums = jnp.dot(
            jnp.concatenate([*parts[0], *parts[1]], axis=0),
            adjacent[...],
            preferred_element_type=jnp.float32,
        )
        across = []
        for f in range(2):
            total = sums[2 * f * rows : (2 * f + 1) * rows] + sums[(2 * f + 1) * rows : (2 * f + 2) * rows]
            across.append((total[:, :128], total[:, 128:]))
    else:
        lane = lax.broadcasted_iota(jnp.int32, (rows, 128), 1)
        across = [neighbours_along_lanes(center[f], lane) for f in range(2)]
    mixed = []
    for f, spread in ((0, FUEL_SPREAD), (1, HEAT_SPREAD)):
        row = []
        for s in range(2):
            view = src.at[f, s, x, pl.ds(start, rows + 2 * PAD), :]
            beside = view[PAD - 1 : PAD - 1 + rows] + view[PAD + 1 : PAD + 1 + rows]
            beside = beside + (
                src[f, s, x - 1, pl.ds(start + PAD, rows), :] + src[f, s, x + 1, pl.ds(start + PAD, rows), :]
            )
            beside = beside + across[f][s]
            row.append((1.0 - 6.0 * spread) * center[f][s] + spread * beside)
        mixed.append(row)
    for s in range(2):
        fuel, heat = mixed[0][s], mixed[1][s]
        inverse = pl.reciprocal(1.0 + heat, approx=False)
        speed = jnp.exp2(ACTIVATION * LOG2E - (ACTIVATION * LOG2E) * inverse)
        burned = rate[s, x - 1, pl.ds(start, rows), :] * fuel * speed
        dst[0, s, x, pl.ds(start + PAD, rows), :] = fuel - burned
        dst[1, s, x, pl.ds(start + PAD, rows), :] = heat + RELEASE * burned


def march(state, x, depth, thickness):
    length = depth // SEGMENTS
    rate = -0.5 * thickness * LOG2E
    sub = lax.broadcasted_iota(jnp.int32, (SEGMENTS, 128), 0)
    halves = []
    for s in range(2):
        rows = lambda f, v: state[f, s, x, pl.ds(PAD + v, SEGMENTS, stride=length), :]
        zero = jnp.zeros((SEGMENTS, 128), jnp.float32)
        red, green, blue, passed = zero, zero, zero, zero
        through = zero + 1.0
        fuel, heat = rows(0, 0), rows(1, 0)
        for v in range(length):
            next_fuel, next_heat = rows(0, v + 1), rows(1, v + 1)
            both_fuel, both_heat = fuel + next_fuel, heat + next_heat
            passed = passed + both_heat
            later = jnp.exp2(rate * passed)
            weight = through - later
            glow = 1.0 - 2.0 * pl.reciprocal(2.0 + both_heat, approx=False)
            shaded = weight * both_fuel
            red = red + weight * glow
            green = green + shaded
            blue = blue + shaded * glow
            through, fuel, heat = later, next_fuel, next_heat
        before = passed
        for by in (1, 2, 4):
            before = before + jnp.where(sub >= by, pltpu.roll(before, by, 0), 0.0)
        share = jnp.exp2(rate * (before - passed))
        halves.append(
            [
                jnp.sum(share * red, axis=0, keepdims=True),
                0.5 * jnp.sum(share * green, axis=0, keepdims=True),
                0.5 * jnp.sum(share * blue, axis=0, keepdims=True),
                (0.5 * thickness) * jnp.sum(passed, axis=0, keepdims=True),
            ]
        )
    return halves


def compose(pieces):
    before = jnp.zeros_like(pieces[0][3])
    total = [jnp.zeros_like(before) for _ in range(3)]
    for piece in pieces:
        share = jnp.exp2(-LOG2E * before)
        total = [t + share * c for t, c in zip(total, piece[:3])]
        before = before + piece[3]
    return total + [1.0 - jnp.exp2(-LOG2E * before)]


def kernel(
    sizes,
    fuel_ref,
    heat_ref,
    rate_ref,
    image_ref,
    fuel_out,
    heat_out,
    even,
    odd,
    rate,
    adjacent,
    colors,
    edge_colors,
    all_colors,
    all_edges,
    in_sem,
    out_sem,
    xs_sem,
    xr_sem,
    zs_sem,
    zr_sem,
    cs_sem,
    cr_sem,
    es_sem,
    er_sem,
):
    devices_x, devices_z, planes, depth, width = sizes
    tx, dz = lax.axis_index("tx"), lax.axis_index("dz")
    thickness = OPACITY / (depth * devices_z)
    buffers = (even, odd)
    chunk = depth // CHUNKS
    last = planes
    has_x = (tx > 0, tx < devices_x - 1)
    has_z = (dz > 0, dz < devices_z - 1)
    to_x = (tx - 1, tx + 1)
    to_z = (dz - 1, dz + 1)

    def load(source, target, k, first, count, at, s):
        return pltpu.make_async_copy(
            source.at[pl.ds(first, count), :, pl.ds(128 * s, 128)], target.at[s, pl.ds(first + at, count)], in_sem.at[k]
        )

    even_rows = [even.at[f, :, :, pl.ds(PAD, depth), :] for f in range(2)]
    edges, k = [], 0
    for x in (0, planes - 1):
        for f, source in ((0, fuel_ref), (1, heat_ref)):
            for s in range(2):
                edges.append(load(source, even_rows[f], k, x, 1, 1, s))
                k += 1
    inner = []
    for f, source in ((0, fuel_ref), (1, heat_ref)):
        for s in range(2):
            inner.append(load(source, even_rows[f], k, 1, planes - 2, 1, s))
            k += 1
    rates = []
    for s in range(2):
        rates.append(load(rate_ref, rate, k, 0, planes, 0, s))
        k += 1
    for copy in edges + inner + rates:
        copy.start()

    for side, plane in ((0, 0), (1, last + 1)):

        @pl.when(jnp.logical_not(has_x[side]))
        def _():
            def clear(r, carry):
                for buffer in buffers:
                    for f in range(2):
                        for s in range(2):
                            buffer[f, s, plane, pl.ds(PAD + r * chunk, chunk), :] = jnp.zeros((chunk, 128), jnp.float32)
                return carry

            lax.fori_loop(0, CHUNKS, clear, 0)

    for side, at in ((0, 0), (1, PAD + depth)):

        @pl.when(jnp.logical_not(has_z[side]))
        def _():
            def clear(x, carry):
                for buffer in buffers:
                    for f in range(2):
                        for s in range(2):
                            buffer[f, s, x, at : at + PAD, :] = jnp.zeros((PAD, 128), jnp.float32)
                return carry

            lax.fori_loop(1, last + 1, clear, 0)

    barrier = pltpu.get_barrier_semaphore()
    for side in range(2):

        @pl.when(has_x[side])
        def _():
            pl.semaphore_signal(barrier, inc=1, device_id={"tx": to_x[side]}, device_id_type=MESH)

    for by in range(1, devices_z):
        peer = lax.rem(dz + by, devices_z)
        pl.semaphore_signal(barrier, inc=1, device_id={"dz": peer}, device_id_type=MESH)

    i = lax.broadcasted_iota(jnp.int32, (width, width), 0)
    j = lax.broadcasted_iota(jnp.int32, (width, width), 1)
    adjacent[...] = jnp.where(jnp.abs(i - j) == 1, 1.0, 0.0).astype(jnp.bfloat16)

    greeted = jnp.where(has_x[0], 1, 0) + jnp.where(has_x[1], 1, 0) + devices_z - 1
    pl.semaphore_wait(barrier, greeted)

    def send_x(par, side, c):
        rows = pl.ds(pl.multiple_of(PAD + c * chunk, 8), chunk)
        mine, theirs = ((1, last + 1), (last, 0))[side]
        return pltpu.make_async_remote_copy(
            src_ref=buffers[par].at[:, :, mine, rows, :],
            dst_ref=buffers[par].at[:, :, theirs, rows, :],
            send_sem=xs_sem.at[par, side, c],
            recv_sem=xr_sem.at[par, side, c],
            device_id={"tx": to_x[side]},
            device_id_type=MESH,
        )

    def send_z(par, side, x):
        mine, theirs = ((PAD, PAD + depth), (depth, 0))[side]
        return pltpu.make_async_remote_copy(
            src_ref=buffers[par].at[:, :, x, pl.ds(mine, PAD), :],
            dst_ref=buffers[par].at[:, :, x, pl.ds(theirs, PAD), :],
            send_sem=zs_sem.at[par, side, x],
            recv_sem=zr_sem.at[par, side, x],
            device_id={"dz": to_z[side]},
            device_id_type=MESH,
        )

    def when(condition, action):
        pl.when(condition)(action)

    def start_z(par, side, x, also=True):
        when(jnp.logical_and(has_z[side], also), lambda: send_z(par, side, x).start())

    def sent_z(par, side, x, also=True):
        when(jnp.logical_and(has_z[side], also), lambda: send_z(par, side, x).wait_send())

    def arrived_z(par, side, x, also=True):
        when(jnp.logical_and(has_z[side], also), lambda: send_z(par, 1 - side, x).wait_recv())

    for copy in edges:
        copy.wait()
    for c in range(CHUNKS):
        for side in range(2):
            when(has_x[side], lambda: send_x(0, side, c).start())
    for x in (1, last):
        for side in range(2):
            start_z(0, side, x)
    for copy in inner:
        copy.wait()

    def begin(x, carry):
        for side in range(2):
            start_z(0, side, x)
        return carry

    lax.fori_loop(2, last, begin, 0)
    for copy in rates:
        copy.wait()

    def edge(step, new, c):
        old = 1 - new
        for side, x in ((0, 1), (1, last)):
            when(has_x[side], lambda: send_x(old, 1 - side, c).wait_recv())
            arrived_z(old, 0, x, c == 0)
            arrived_z(old, 1, x, c == CHUNKS - 1)
            again = step >= 2
            when(jnp.logical_and(has_x[side], again), lambda: send_x(new, side, c).wait_send())
            sent_z(new, 0, x, jnp.logical_and(c == 0, again))
            sent_z(new, 1, x, jnp.logical_and(c == CHUNKS - 1, again))
            advance(buffers[old], buffers[new], rate, adjacent, x, pl.multiple_of(c * chunk, chunk), chunk, False)
            when(jnp.logical_and(has_x[side], step < STEPS), lambda: send_x(new, side, c).start())
            start_z(new, 0, x, c == 0)
            start_z(new, 1, x, jnp.logical_and(c == CHUNKS - 1, step < STEPS))

    def interior(step, new, low, high):
        old = 1 - new

        def plane(x, carry):
            for side in range(2):
                arrived_z(old, side, x)
                sent_z(new, side, x, step >= 2)
            advance(buffers[old], buffers[new], rate, adjacent, x, 0, depth, True)
            start_z(new, 0, x)
            start_z(new, 1, x, step < STEPS)
            return carry

        lax.fori_loop(low, high, plane, 0)

    def written(x, f, s):
        target = (fuel_out, heat_out)[f]
        return pltpu.make_async_copy(
            even.at[f, s, x, pl.ds(PAD, depth), :], target.at[x - 1, :, pl.ds(128 * s, 128)], out_sem.at[x - 1, f, s]
        )

    def render(x):
        for f in range(2):
            for s in range(2):
                written(x, f, s).start()
        arrived_z(0, 1, x)
        return march(even, x, depth, thickness)

    def send_colors(by):
        peer = lax.rem(dz + by, devices_z)
        return pltpu.make_async_remote_copy(
            src_ref=colors.at[peer // (devices_z // 2)],
            dst_ref=all_colors.at[dz],
            send_sem=cs_sem.at[by],
            recv_sem=cr_sem.at[by],
            device_id={"dz": peer},
            device_id_type=MESH,
        )

    def send_edges(by):
        peer = lax.rem(dz + by, devices_z)
        return pltpu.make_async_remote_copy(
            src_ref=edge_colors.at[peer // (devices_z // 2)],
            dst_ref=all_edges.at[dz],
            send_sem=es_sem.at[by],
            recv_sem=er_sem.at[by],
            device_id={"dz": peer},
            device_id_type=MESH,
        )

    def render_inner(i, carry):
        x = jnp.where(i < 8, i + 5, jnp.where(i < 11, i - 6, i + 2))
        for s, channels in enumerate(render(x)):
            for ch, value in enumerate(channels):
                colors[s, ch, pl.ds(x - 1, 1), :] = value
        return carry

    mine = dz // (devices_z // 2)
    interior(1, 1, 5, 13)

    def pair(it, carry):
        for new in (1, 0):
            step = 2 * it + (1 if new else 2)

            def early(c, carry, new=new, step=step):
                edge(step, new, c)
                interior(step, new, 2 + 11 * c, 5 + 11 * c)
                if new == 0:
                    when(step == STEPS, lambda: lax.fori_loop(4 * c, 4 * c + 4, render_inner, None) and None)
                return carry

            lax.fori_loop(0, 2, early, 0)

            def late(c, carry, new=new, step=step):
                edge(step, new, c)
                if new == 0:

                    @pl.when(step < STEPS)
                    def _():
                        interior(step + 1, 1 - new, 4 * c - 3, 4 * c + 1)

                    @pl.when(jnp.logical_and(step == STEPS, c == 2))
                    def _():
                        lax.fori_loop(8, planes - 2, render_inner, None)
                        for by in range(1, devices_z):
                            send_colors(by).start()
                        all_colors[dz] = colors[mine]
                else:
                    interior(step + 1, 1 - new, 4 * c - 3, 4 * c + 1)
                return carry

            lax.fori_loop(2, 4, late, 0)
        return carry

    lax.fori_loop(0, STEPS // 2, pair, 0)

    for e, x in ((0, 1), (1, last)):
        for s, channels in enumerate(render(x)):
            for ch, value in enumerate(channels):
                edge_colors[s, 2 * ch + e : 2 * ch + e + 1, :] = value
    for by in range(1, devices_z):
        send_edges(by).start()
    all_edges[dz] = edge_colors[mine]

    share = width // devices_z
    shift = lax.rem(128 - share * lax.rem(dz, devices_z // 2), 128)
    for by in range(1, devices_z):
        send_colors(by).wait_recv()
    image = compose([[all_colors[b, ch] for ch in range(4)] for b in range(devices_z)])
    for ch in range(4):
        image_ref[ch] = pltpu.roll(image[ch], shift, 1)[:, :share]
    for by in range(1, devices_z):
        send_edges(by).wait_recv()
    image = compose([[all_edges[b, 2 * ch : 2 * ch + 2, :] for ch in range(4)] for b in range(devices_z)])
    for ch in range(4):
        value = pltpu.roll(image[ch], shift, 1)[:, :share]
        image_ref[ch, 0:1] = value[0:1]
        image_ref[ch, planes - 1 : planes] = value[1:2]

    for by in range(1, devices_z):
        send_colors(by).wait_send()
        send_edges(by).wait_send()
    for c in range(CHUNKS):
        for side in range(2):
            when(has_x[side], lambda: send_x(1, side, c).wait_send())

    def finish(x, carry):
        sent_z(1, 0, x)
        sent_z(1, 1, x)
        sent_z(0, 0, x)
        for f in range(2):
            for s in range(2):
                written(x, f, s).wait()
        return carry

    lax.fori_loop(1, last + 1, finish, 0)


def body(fuel, heat, rate):
    planes, depth, width = fuel.shape
    devices_x, devices_z = lax.axis_size("tx"), lax.axis_size("dz")
    sizes = (devices_x, devices_z, planes, depth, width)
    anywhere = pl.BlockSpec(memory_space=pl.ANY)
    block = pltpu.VMEM((2, 2, planes + 2, depth + 2 * PAD, 128), jnp.float32)
    dma = pltpu.SemaphoreType.DMA
    return pl.pallas_call(
        functools.partial(kernel, sizes),
        out_shape=(
            jax.ShapeDtypeStruct((4, planes, width // devices_z), jnp.float32),
            jax.ShapeDtypeStruct(fuel.shape, jnp.float32),
            jax.ShapeDtypeStruct(fuel.shape, jnp.float32),
        ),
        in_specs=[anywhere] * 3,
        out_specs=(pl.BlockSpec(memory_space=pltpu.VMEM), anywhere, anywhere),
        scratch_shapes=[
            block,
            block,
            pltpu.VMEM((2, planes, depth, 128), jnp.float32),
            pltpu.VMEM((width, width), jnp.bfloat16),
            pltpu.VMEM((2, 4, planes, 128), jnp.float32),
            pltpu.VMEM((2, 8, 128), jnp.float32),
            pltpu.VMEM((devices_z, 4, planes, 128), jnp.float32),
            pltpu.VMEM((devices_z, 8, 128), jnp.float32),
            dma((14,)),
            dma((planes, 2, 2)),
            dma((2, 2, CHUNKS)),
            dma((2, 2, CHUNKS)),
            dma((2, 2, planes + 2)),
            dma((2, 2, planes + 2)),
            dma((devices_z,)),
            dma((devices_z,)),
            dma((devices_z,)),
            dma((devices_z,)),
        ],
        compiler_params=pltpu.CompilerParams(
            collective_id=0, has_side_effects=True, vmem_limit_bytes=56 * 2**20
        ),
    )(fuel, heat, rate)


def solution(mesh):
    placed = (P("tx", "dz", None),) * 3
    return jax.shard_map(
        body,
        mesh=mesh,
        in_specs=placed,
        out_specs=(P(None, "tx", "dz"), P("tx", "dz", None), P("tx", "dz", None)),
        check_vma=False,
    )
```

```python
import functools

import jax
import jax.numpy as jnp
from jax import lax
from jax.experimental import pallas as pl
from jax.experimental.pallas import tpu as pltpu
from jax.sharding import PartitionSpec as P

STEPS = 4
FUEL_SPREAD = 0.15
HEAT_SPREAD = 0.12
ACTIVATION = 1.5
RELEASE = 2.0
OPACITY = 1.5
LOG2E = 1.4426950408889634
MESH = pl.DeviceIdType.MESH

PAD = 8
ROWS_AFTER = 24
CHUNKS = 4
SEGMENTS = 8
GROUPS = (((2, 1), (15, 1)), ((3, 6),), ((9, 6),), ((1, 1), (16, 1)))
BESIDE, LOWER, UPPER, EDGES = range(4)


def neighbours_along_lanes(halves, lane):
    first, last = lane == 0, lane == 127
    low, high = halves
    zero = jnp.zeros_like(low)
    up_low, up_high = pltpu.roll(low, 1, 1), pltpu.roll(high, 1, 1)
    down_low, down_high = pltpu.roll(low, 127, 1), pltpu.roll(high, 127, 1)
    return (
        jnp.where(first, zero, up_low) + jnp.where(last, down_high, down_low),
        jnp.where(first, up_low, up_high) + jnp.where(last, zero, down_high),
    )


def split(value):
    high = value.astype(jnp.bfloat16)
    low = (value - high.astype(jnp.float32)).astype(jnp.bfloat16)
    return high, low


def advance(src, dst, rate, adjacent, x, start, rows, matrix):
    center = [[src[f, s, x, pl.ds(start + PAD, rows), :] for s in range(2)] for f in range(2)]
    if matrix:
        parts = [split(jnp.concatenate(center[f], axis=1)) for f in range(2)]
        sums = jnp.dot(
            jnp.concatenate([*parts[0], *parts[1]], axis=0),
            adjacent[...],
            preferred_element_type=jnp.float32,
        )
        across = []
        for f in range(2):
            total = sums[2 * f * rows : (2 * f + 1) * rows] + sums[(2 * f + 1) * rows : (2 * f + 2) * rows]
            across.append((total[:, :128], total[:, 128:]))
    else:
        lane = lax.broadcasted_iota(jnp.int32, (rows, 128), 1)
        across = [neighbours_along_lanes(center[f], lane) for f in range(2)]
    mixed = []
    for f, spread in ((0, FUEL_SPREAD), (1, HEAT_SPREAD)):
        row = []
        for s in range(2):
            view = src.at[f, s, x, pl.ds(start, rows + 2 * PAD), :]
            beside = view[PAD - 1 : PAD - 1 + rows] + view[PAD + 1 : PAD + 1 + rows]
            beside = beside + (
                src[f, s, x - 1, pl.ds(start + PAD, rows), :] + src[f, s, x + 1, pl.ds(start + PAD, rows), :]
            )
            beside = beside + across[f][s]
            row.append((1.0 - 6.0 * spread) * center[f][s] + spread * beside)
        mixed.append(row)
    for s in range(2):
        fuel, heat = mixed[0][s], mixed[1][s]
        inverse = pl.reciprocal(1.0 + heat, approx=False)
        speed = jnp.exp2(ACTIVATION * LOG2E - (ACTIVATION * LOG2E) * inverse)
        burned = rate[s, x - 1, pl.ds(start, rows), :] * fuel * speed
        dst[0, s, x, pl.ds(start + PAD, rows), :] = fuel - burned
        dst[1, s, x, pl.ds(start + PAD, rows), :] = heat + RELEASE * burned


def march(state, planes, depth, thickness):
    length = depth // SEGMENTS + 1
    full = depth - (SEGMENTS - 1) * length
    rate = -0.5 * thickness * LOG2E
    sub = lax.broadcasted_iota(jnp.int32, (SEGMENTS, 128), 0)
    zero = jnp.zeros((SEGMENTS, 128), jnp.float32)
    halves = []
    for x in planes:
        for s in range(2):
            rows = lambda f, v: state[f, s, x, pl.ds(PAD + v, SEGMENTS, stride=length), :]
            red, green, blue, passed = zero, zero, zero, zero
            through = zero + 1.0
            fuel, heat = rows(0, 0), rows(1, 0)
            for v in range(length):
                next_fuel, next_heat = rows(0, v + 1), rows(1, v + 1)
                both_fuel, both_heat = fuel + next_fuel, heat + next_heat
                if v >= full:
                    both_heat = jnp.where(sub < SEGMENTS - 1, both_heat, 0.0)
                passed = passed + both_heat
                later = jnp.exp2(rate * passed)
                weight = through - later
                glow = 1.0 - 2.0 * pl.reciprocal(2.0 + both_heat, approx=False)
                shaded = weight * both_fuel
                red = red + weight * glow
                green = green + shaded
                blue = blue + shaded * glow
                through, fuel, heat = later, next_fuel, next_heat
            before = passed
            for by in (1, 2, 4):
                before = before + jnp.where(sub >= by, pltpu.roll(before, by, 0), 0.0)
            share = jnp.exp2(rate * (before - passed))
            halves.append(
                [
                    jnp.sum(share * red, axis=0, keepdims=True),
                    0.5 * jnp.sum(share * green, axis=0, keepdims=True),
                    0.5 * jnp.sum(share * blue, axis=0, keepdims=True),
                    (0.5 * thickness) * jnp.sum(passed, axis=0, keepdims=True),
                ]
            )
    return halves


def compose(pieces):
    before = jnp.zeros_like(pieces[0][3])
    total = [jnp.zeros_like(before) for _ in range(3)]
    for piece in pieces:
        share = jnp.exp2(-LOG2E * before)
        total = [t + share * c for t, c in zip(total, piece[:3])]
        before = before + piece[3]
    return total + [1.0 - jnp.exp2(-LOG2E * before)]


def kernel(
    sizes,
    fuel_ref,
    heat_ref,
    rate_ref,
    even,
    all_colors,
    all_edges,
    odd,
    rate,
    adjacent,
    colors,
    edge_colors,
    in_sem,
    xs_sem,
    xr_sem,
    zs_sem,
    zr_sem,
    cs_sem,
    cr_sem,
    es_sem,
    er_sem,
):
    devices_x, devices_z, planes, depth, width = sizes
    tx, dz = lax.axis_index("tx"), lax.axis_index("dz")
    thickness = OPACITY / (depth * devices_z)
    buffers = (even, odd)
    chunk = depth // CHUNKS
    last = planes
    has_x = (tx > 0, tx < devices_x - 1)
    has_z = (dz > 0, dz < devices_z - 1)
    to_x = (tx - 1, tx + 1)
    to_z = (dz - 1, dz + 1)

    def load(source, target, k, first, count, at, s):
        return pltpu.make_async_copy(
            source.at[pl.ds(first, count), :, pl.ds(128 * s, 128)], target.at[s, pl.ds(first + at, count)], in_sem.at[k]
        )

    even_rows = [even.at[f, :, :, pl.ds(PAD, depth), :] for f in range(2)]
    fields = ((0, fuel_ref), (1, heat_ref))
    edges = [load(r, even_rows[f], 0, x, 1, 1, s) for x in (0, planes - 1) for f, r in fields for s in range(2)]
    inner = [load(r, even_rows[f], 1, 1, planes - 2, 1, s) for f, r in fields for s in range(2)]
    rates = [load(rate_ref, rate, 2, 0, planes, 0, s) for s in range(2)]

    def landed(k, block):
        pltpu.make_async_copy(block, block, in_sem.at[k]).wait()

    for copy in edges + inner + rates:
        copy.start()

    for side, plane in ((0, 0), (1, last + 1)):

        @pl.when(jnp.logical_not(has_x[side]))
        def _():
            def clear(r, carry):
                for buffer in buffers:
                    for f in range(2):
                        for s in range(2):
                            buffer[f, s, plane, pl.ds(PAD + r * chunk, chunk), :] = jnp.zeros((chunk, 128), jnp.float32)
                return carry

            lax.fori_loop(0, CHUNKS, clear, 0)

    for side, at in ((0, 0), (1, PAD + depth)):

        @pl.when(jnp.logical_not(has_z[side]))
        def _():
            def clear(x, carry):
                for buffer in buffers:
                    for f in range(2):
                        for s in range(2):
                            buffer[f, s, x, at : at + PAD, :] = jnp.zeros((PAD, 128), jnp.float32)
                return carry

            lax.fori_loop(1, last + 1, clear, 0)

    barrier = pltpu.get_barrier_semaphore()
    for side in range(2):

        @pl.when(has_x[side])
        def _():
            pl.semaphore_signal(barrier, inc=1, device_id={"tx": to_x[side]}, device_id_type=MESH)

    for by in range(1, devices_z):
        peer = lax.rem(dz + by, devices_z)
        pl.semaphore_signal(barrier, inc=1, device_id={"dz": peer}, device_id_type=MESH)

    def clear_after(x, carry):
        for f in range(2):
            for s in range(2):
                even[f, s, x, depth + 2 * PAD :, :] = jnp.zeros((PAD, 128), jnp.float32)
        return carry

    lax.fori_loop(1, last + 1, clear_after, 0)
    i = lax.broadcasted_iota(jnp.int32, (width, width), 0)
    j = lax.broadcasted_iota(jnp.int32, (width, width), 1)
    adjacent[...] = jnp.where(jnp.abs(i - j) == 1, 1.0, 0.0).astype(jnp.bfloat16)

    greeted = jnp.where(has_x[0], 1, 0) + jnp.where(has_x[1], 1, 0) + devices_z - 1
    pl.semaphore_wait(barrier, greeted)

    def send_x(par, side, c, count=1):
        rows = pl.ds(pl.multiple_of(PAD + c * chunk, 8), count * chunk)
        mine, theirs = ((1, last + 1), (last, 0))[side]
        return pltpu.make_async_remote_copy(
            src_ref=buffers[par].at[:, :, mine, rows, :],
            dst_ref=buffers[par].at[:, :, theirs, rows, :],
            send_sem=xs_sem.at[par, side],
            recv_sem=xr_sem.at[par, side, c],
            device_id={"tx": to_x[side]},
            device_id_type=MESH,
        )

    def send_z(par, side, group, first, count):
        mine, theirs = ((PAD, PAD + depth), (depth, 0))[side]
        return pltpu.make_async_remote_copy(
            src_ref=buffers[par].at[:, :, pl.ds(first, count), pl.ds(mine, PAD), :],
            dst_ref=buffers[par].at[:, :, pl.ds(first, count), pl.ds(theirs, PAD), :],
            send_sem=zs_sem.at[par, side],
            recv_sem=zr_sem.at[par, side, group],
            device_id={"dz": to_z[side]},
            device_id_type=MESH,
        )

    def when(condition, action):
        pl.when(condition)(action)

    def start_x(par, side, c, also=True):
        when(jnp.logical_and(has_x[side], also), lambda: send_x(par, side, c).start())

    def sent_x(par, side, also=True):
        when(jnp.logical_and(has_x[side], also), lambda: send_x(par, side, 0, CHUNKS).wait_send())

    def start_z(par, side, group, also=True):
        def start():
            for first, count in GROUPS[group]:
                send_z(par, side, group, first, count).start()

        when(jnp.logical_and(has_z[side], also), start)

    def sent_z(par, side, also=True):
        when(jnp.logical_and(has_z[side], also), lambda: send_z(par, side, 0, 1, planes).wait_send())

    def arrived_z(par, side, group, also=True):
        count = sum(count for _, count in GROUPS[group])
        when(jnp.logical_and(has_z[side], also), lambda: send_z(par, 1 - side, group, 1, count).wait_recv())

    def both(action, *args):
        for side in range(2):
            action(args[0], side, *args[1:])

    landed(0, even.at[:, :, pl.ds(1, 2), pl.ds(PAD, depth), :])
    for c in range(CHUNKS):
        both(start_x, 0, c)
    both(start_z, 0, EDGES)
    landed(1, even.at[:, :, pl.ds(1, planes - 2), pl.ds(PAD, depth), :])
    for group in (LOWER, UPPER, BESIDE):
        both(start_z, 0, group)
    landed(2, rate)

    def edge(step, new, c):
        old = 1 - new
        ahead = step < STEPS
        arrived_z(old, 0, EDGES, c == 0)
        arrived_z(old, 1, EDGES, c == CHUNKS - 1)
        for side, x in ((0, 1), (1, last)):
            when(has_x[side], lambda: send_x(old, 1 - side, c).wait_recv())
            sent_x(new, side, jnp.logical_and(c == 0, step >= 2))
            advance(buffers[old], buffers[new], rate, adjacent, x, pl.multiple_of(c * chunk, chunk), chunk, False)
            start_x(new, side, c, ahead)
        start_z(new, 0, EDGES, c == 0)
        start_z(new, 1, EDGES, jnp.logical_and(c == CHUNKS - 1, ahead))

    def interior(new, low, high, stride=1):
        def plane(i, carry):
            advance(buffers[1 - new], buffers[new], rate, adjacent, low + i * stride, 0, depth, True)
            return carry

        lax.fori_loop(0, (high - low + stride - 1) // stride, plane, 0)

    def ahead_of(step, new, c):
        old = 1 - new
        if not isinstance(c, int):
            pl.when(c == 2)(lambda: both(arrived_z, old, UPPER))
            interior(new, 4 * c + 1, 4 * c + 5)

            @pl.when(c == 1)
            def _():
                start_z(new, 0, LOWER)
                start_z(new, 1, LOWER, step + 1 < STEPS)

        elif c == 0:
            both(arrived_z, old, LOWER)
            both(sent_z, new)
            interior(new, 3, 5)
        else:
            interior(new, 13, 15)
            start_z(new, 0, UPPER)
            start_z(new, 1, UPPER, step + 1 < STEPS)

    def send_colors(by, source, target, send_sem, recv_sem):
        peer = lax.rem(dz + by, devices_z)
        return pltpu.make_async_remote_copy(
            src_ref=source.at[peer // (devices_z // 2)],
            dst_ref=target.at[dz],
            send_sem=send_sem.at[0],
            recv_sem=recv_sem.at[0],
            device_id={"dz": peer},
            device_id_type=MESH,
        )

    def share_colors(source, target, send_sem, recv_sem):
        for by in range(1, devices_z):
            send_colors(by, source, target, send_sem, recv_sem).start()
        target[dz] = source[dz // (devices_z // 2)]

    def shared_colors(source, target, send_sem, recv_sem):
        all_peers = target.at[pl.ds(0, devices_z - 1)]
        pltpu.make_async_copy(all_peers, all_peers, recv_sem.at[0]).wait()
        pltpu.make_async_copy(all_peers, all_peers, send_sem.at[0]).wait()

    inner_way = (colors, all_colors, cs_sem, cr_sem)
    edge_way = (edge_colors, all_edges, es_sem, er_sem)

    def render(low, high, stride=1):
        def plane(i, carry):
            x = low + i * stride
            for s, channels in enumerate(march(even, (x,), depth, thickness)):
                for ch, value in enumerate(channels):
                    colors[s, ch, pl.ds(x - 1, 1), :] = value
            return carry

        lax.fori_loop(0, (high - low + stride - 1) // stride, plane, 0)

    both(arrived_z, 0, LOWER)
    interior(1, 3, 9)
    both(start_z, 1, LOWER)
    both(arrived_z, 0, UPPER)
    interior(1, 9, 15)
    both(start_z, 1, UPPER)

    def pair(it, carry):
        for new in (1, 0):
            step = 2 * it + (1 if new else 2)
            final = step == STEPS
            ahead = step < STEPS
            old = 1 - new

            edge(step, new, 0)
            both(arrived_z, old, BESIDE)
            interior(new, 2, 16, 13)
            start_z(new, 0, BESIDE)
            start_z(new, 1, BESIDE, ahead)
            if new:
                ahead_of(step, 0, 0)
            else:
                pl.when(ahead)(lambda: ahead_of(step, 1, 0))

                @pl.when(final)
                def _():
                    arrived_z(0, 1, UPPER)
                    render(9, 13)

            def middle(c, carry, new=new, step=step, final=final, ahead=ahead):
                edge(step, new, c)
                if new:
                    ahead_of(step, 0, c)

                    @pl.when(jnp.logical_and(it == 1, c == 2))
                    def _():
                        arrived_z(0, 1, LOWER)
                        render(3, 5)

                else:
                    pl.when(ahead)(lambda: ahead_of(step, 1, c))

                    @pl.when(jnp.logical_and(final, c == 1))
                    def _():
                        render(13, 15)
                        arrived_z(0, 1, BESIDE)
                        render(2, 16, 13)
                        share_colors(*inner_way)

                return carry

            lax.fori_loop(1, 3, middle, 0)

            edge(step, new, 3)
            if new:
                ahead_of(step, 0, 3)
                pl.when(it == 1)(lambda: render(5, 9))
            else:
                pl.when(ahead)(lambda: ahead_of(step, 1, 3))
        return carry

    lax.fori_loop(0, STEPS // 2, pair, 0)

    arrived_z(0, 1, EDGES)
    for k, channels in enumerate(march(even, (1, last), depth, thickness)):
        e, s = k // 2, k % 2
        for ch, value in enumerate(channels):
            edge_colors[s, 2 * ch + e : 2 * ch + e + 1, :] = value
    share_colors(*edge_way)

    both(sent_x, 1)
    both(sent_z, 1)
    sent_z(0, 0)
    shared_colors(*inner_way)
    shared_colors(*edge_way)


def results(state, all_colors, all_edges, image_out, fuel_out, heat_out, image_ref, sem, image_sem):
    devices_z, _, planes, _ = all_colors.shape
    depth = fuel_out.shape[1]
    share = image_ref.shape[2]
    dz = lax.axis_index("dz")
    copies = [
        pltpu.make_async_copy(
            state.at[f, s, pl.ds(1, planes), pl.ds(PAD, depth), :], target.at[:, :, pl.ds(128 * s, 128)], sem.at[f, s]
        )
        for f, target in ((0, fuel_out), (1, heat_out))
        for s in range(2)
    ]
    for copy in copies:
        copy.start()
    shift = lax.rem(128 - share * lax.rem(dz, devices_z // 2), 128)
    image = compose([[all_colors[b, ch] for ch in range(4)] for b in range(devices_z)])
    for ch in range(4):
        image_ref[ch] = pltpu.roll(image[ch], shift, 1)[:, :share]
    image = compose([[all_edges[b, 2 * ch : 2 * ch + 2, :] for ch in range(4)] for b in range(devices_z)])
    for ch in range(4):
        value = pltpu.roll(image[ch], shift, 1)[:, :share]
        image_ref[ch, 0:1] = value[0:1]
        image_ref[ch, planes - 1 : planes] = value[1:2]
    copies.append(pltpu.make_async_copy(image_ref, image_out, image_sem))
    copies[-1].start()
    for copy in copies:
        copy.wait()


def body(fuel, heat, rate):
    planes, depth, width = fuel.shape
    devices_x, devices_z = lax.axis_size("tx"), lax.axis_size("dz")
    sizes = (devices_x, devices_z, planes, depth, width)
    anywhere = pl.BlockSpec(memory_space=pltpu.HBM)
    local = pl.BlockSpec(memory_space=pltpu.VMEM)
    block = pltpu.VMEM((2, 2, planes + 2, depth + ROWS_AFTER, 128), jnp.float32)
    dma = pltpu.SemaphoreType.DMA
    arrived = pl.pallas_call(
        functools.partial(kernel, sizes),
        out_shape=(
            block,
            pltpu.VMEM((devices_z, 4, planes, 128), jnp.float32),
            pltpu.VMEM((devices_z, 8, 128), jnp.float32),
        ),
        in_specs=[anywhere] * 3,
        out_specs=(local,) * 3,
        scratch_shapes=[
            block,
            pltpu.VMEM((2, planes, depth, 128), jnp.float32),
            pltpu.VMEM((width, width), jnp.bfloat16),
            pltpu.VMEM((2, 4, planes, 128), jnp.float32),
            pltpu.VMEM((2, 8, 128), jnp.float32),
            dma((3,)),
            dma((2, 2)),
            dma((2, 2, CHUNKS)),
            dma((2, 2)),
            dma((2, 2, len(GROUPS))),
            dma((1,)),
            dma((1,)),
            dma((1,)),
            dma((1,)),
        ],
        compiler_params=pltpu.CompilerParams(
            collective_id=0, has_side_effects=True, vmem_limit_bytes=40 * 2**20
        ),
    )(*(pltpu.with_memory_space_constraint(a, pltpu.HBM) for a in (fuel, heat, rate)))
    return pl.pallas_call(
        results,
        out_shape=(
            jax.ShapeDtypeStruct((4, planes, width // devices_z), jnp.float32),
            jax.ShapeDtypeStruct(fuel.shape, jnp.float32),
            jax.ShapeDtypeStruct(fuel.shape, jnp.float32),
        ),
        in_specs=[local] * 3,
        out_specs=(anywhere,) * 3,
        scratch_shapes=[
            pltpu.VMEM((4, planes, width // devices_z), jnp.float32),
            dma((2, 2)),
            dma,
        ],
        compiler_params=pltpu.CompilerParams(vmem_limit_bytes=40 * 2**20),
    )(*arrived)


def solution(mesh):
    placed = (P("tx", "dz", None),) * 3
    return jax.shard_map(
        body,
        mesh=mesh,
        in_specs=placed,
        out_specs=(P(None, "tx", "dz"), P("tx", "dz", None), P("tx", "dz", None)),
        check_vma=False,
    )
```

```python
import functools

import jax
import jax.numpy as jnp
from jax import lax
from jax.experimental import pallas as pl
from jax.experimental.pallas import tpu as pltpu
from jax.sharding import PartitionSpec as P

STEPS = 4
FUEL_SPREAD = 0.15
HEAT_SPREAD = 0.12
ACTIVATION = 1.5
RELEASE = 2.0
OPACITY = 1.5
LOG2E = 1.4426950408889634
MESH = pl.DeviceIdType.MESH

PAD = 8
ROWS_AFTER = 24
CHUNKS = 4
SEGMENTS = 8
GROUPS = (((2, 1), (15, 1)), ((3, 6),), ((9, 6),), ((1, 1), (16, 1)))
BESIDE, LOWER, UPPER, EDGES = range(4)


def neighbours_along_lanes(halves, lane):
    first, last = lane == 0, lane == 127
    low, high = halves
    zero = jnp.zeros_like(low)
    up_low, up_high = pltpu.roll(low, 1, 1), pltpu.roll(high, 1, 1)
    down_low, down_high = pltpu.roll(low, 127, 1), pltpu.roll(high, 127, 1)
    return (
        jnp.where(first, zero, up_low) + jnp.where(last, down_high, down_low),
        jnp.where(first, up_low, up_high) + jnp.where(last, zero, down_high),
    )


def split(value):
    high = value.astype(jnp.bfloat16)
    low = (value - high.astype(jnp.float32)).astype(jnp.bfloat16)
    return high, low


def advance(src, dst, rate, adjacent, x, start, rows, matrix):
    center = [[src[f, s, x, pl.ds(start + PAD, rows), :] for s in range(2)] for f in range(2)]
    if matrix:
        parts = [split(jnp.concatenate(center[f], axis=1)) for f in range(2)]
        sums = jnp.dot(
            jnp.concatenate([*parts[0], *parts[1]], axis=0),
            adjacent[...],
            preferred_element_type=jnp.float32,
        )
        across = []
        for f in range(2):
            total = sums[2 * f * rows : (2 * f + 1) * rows] + sums[(2 * f + 1) * rows : (2 * f + 2) * rows]
            across.append((total[:, :128], total[:, 128:]))
    else:
        lane = lax.broadcasted_iota(jnp.int32, (rows, 128), 1)
        across = [neighbours_along_lanes(center[f], lane) for f in range(2)]
    mixed = []
    for f, spread in ((0, FUEL_SPREAD), (1, HEAT_SPREAD)):
        row = []
        for s in range(2):
            view = src.at[f, s, x, pl.ds(start, rows + 2 * PAD), :]
            beside = view[PAD - 1 : PAD - 1 + rows] + view[PAD + 1 : PAD + 1 + rows]
            beside = beside + (
                src[f, s, x - 1, pl.ds(start + PAD, rows), :] + src[f, s, x + 1, pl.ds(start + PAD, rows), :]
            )
            beside = beside + across[f][s]
            row.append((1.0 - 6.0 * spread) * center[f][s] + spread * beside)
        mixed.append(row)
    for s in range(2):
        fuel, heat = mixed[0][s], mixed[1][s]
        inverse = pl.reciprocal(1.0 + heat, approx=False)
        speed = jnp.exp2(ACTIVATION * LOG2E - (ACTIVATION * LOG2E) * inverse)
        burned = rate[s, x - 1, pl.ds(start, rows), :] * fuel * speed
        dst[0, s, x, pl.ds(start + PAD, rows), :] = fuel - burned
        dst[1, s, x, pl.ds(start + PAD, rows), :] = heat + RELEASE * burned


def march(state, planes, depth, thickness):
    length = depth // SEGMENTS + 1
    full = depth - (SEGMENTS - 1) * length
    rate = -0.5 * thickness * LOG2E
    sub = lax.broadcasted_iota(jnp.int32, (SEGMENTS, 128), 0)
    zero = jnp.zeros((SEGMENTS, 128), jnp.float32)
    halves = []
    for x in planes:
        for s in range(2):
            rows = lambda f, v: state[f, s, x, pl.ds(PAD + v, SEGMENTS, stride=length), :]
            red, green, blue, passed = zero, zero, zero, zero
            through = zero + 1.0
            fuel, heat = rows(0, 0), rows(1, 0)
            for v in range(length):
                next_fuel, next_heat = rows(0, v + 1), rows(1, v + 1)
                both_fuel, both_heat = fuel + next_fuel, heat + next_heat
                if v >= full:
                    both_fuel = jnp.where(sub < SEGMENTS - 1, both_fuel, 0.0)
                    both_heat = jnp.where(sub < SEGMENTS - 1, both_heat, 0.0)
                passed = passed + both_heat
                later = jnp.exp2(rate * passed)
                weight = through - later
                glow = 1.0 - 2.0 * pl.reciprocal(2.0 + both_heat, approx=False)
                shaded = weight * both_fuel
                red = red + weight * glow
                green = green + shaded
                blue = blue + shaded * glow
                through, fuel, heat = later, next_fuel, next_heat
            before = passed
            for by in (1, 2, 4):
                before = before + jnp.where(sub >= by, pltpu.roll(before, by, 0), 0.0)
            share = jnp.exp2(rate * (before - passed))
            halves.append(
                [
                    jnp.sum(share * red, axis=0, keepdims=True),
                    0.5 * jnp.sum(share * green, axis=0, keepdims=True),
                    0.5 * jnp.sum(share * blue, axis=0, keepdims=True),
                    (0.5 * thickness) * jnp.sum(passed, axis=0, keepdims=True),
                ]
            )
    return halves


def compose(pieces):
    before = jnp.zeros_like(pieces[0][3])
    total = [jnp.zeros_like(before) for _ in range(3)]
    for piece in pieces:
        share = jnp.exp2(-LOG2E * before)
        total = [t + share * c for t, c in zip(total, piece[:3])]
        before = before + piece[3]
    return total + [1.0 - jnp.exp2(-LOG2E * before)]


def kernel(
    sizes,
    fuel_ref,
    heat_ref,
    rate_ref,
    even,
    all_colors,
    all_edges,
    odd,
    rate,
    adjacent,
    colors,
    edge_colors,
    in_sem,
    xs_sem,
    xr_sem,
    zs_sem,
    zr_sem,
    cs_sem,
    cr_sem,
    es_sem,
    er_sem,
):
    devices_x, devices_z, planes, depth, width = sizes
    tx, dz = lax.axis_index("tx"), lax.axis_index("dz")
    thickness = OPACITY / (depth * devices_z)
    buffers = (even, odd)
    chunk = depth // CHUNKS
    last = planes
    has_x = (tx > 0, tx < devices_x - 1)
    has_z = (dz > 0, dz < devices_z - 1)
    to_x = (tx - 1, tx + 1)
    to_z = (dz - 1, dz + 1)

    barrier = pltpu.get_barrier_semaphore()
    for side in range(2):

        @pl.when(has_x[side])
        def _():
            pl.semaphore_signal(barrier, inc=1, device_id={"tx": to_x[side]}, device_id_type=MESH)

    for by in range(1, devices_z):
        peer = lax.rem(dz + by, devices_z)
        pl.semaphore_signal(barrier, inc=1, device_id={"dz": peer}, device_id_type=MESH)

    def load(source, target, k, first, count, at, s):
        return pltpu.make_async_copy(
            source.at[pl.ds(first, count), :, pl.ds(128 * s, 128)], target.at[s, pl.ds(first + at, count)], in_sem.at[k]
        )

    even_rows = [even.at[f, :, :, pl.ds(PAD, depth), :] for f in range(2)]
    fields = ((0, fuel_ref), (1, heat_ref))
    edges = [load(r, even_rows[f], 0, x, 1, 1, s) for x in (0, planes - 1) for f, r in fields for s in range(2)]
    inner = [load(r, even_rows[f], 1, 1, planes - 2, 1, s) for f, r in fields for s in range(2)]
    rates = [load(rate_ref, rate, 2, 0, planes, 0, s) for s in range(2)]

    def landed(k, block):
        pltpu.make_async_copy(block, block, in_sem.at[k]).wait()

    for copy in edges + inner + rates:
        copy.start()

    for side, plane in ((0, 0), (1, last + 1)):

        @pl.when(jnp.logical_not(has_x[side]))
        def _():
            def clear(r, carry):
                for buffer in buffers:
                    for f in range(2):
                        for s in range(2):
                            buffer[f, s, plane, pl.ds(PAD + r * chunk, chunk), :] = jnp.zeros((chunk, 128), jnp.float32)
                return carry

            lax.fori_loop(0, CHUNKS, clear, 0)

    for side, at in ((0, 0), (1, PAD + depth)):

        @pl.when(jnp.logical_not(has_z[side]))
        def _():
            def clear(x, carry):
                for buffer in buffers:
                    for f in range(2):
                        for s in range(2):
                            buffer[f, s, x, at : at + PAD, :] = jnp.zeros((PAD, 128), jnp.float32)
                return carry

            lax.fori_loop(1, last + 1, clear, 0)

    i = lax.broadcasted_iota(jnp.int32, (width, width), 0)
    j = lax.broadcasted_iota(jnp.int32, (width, width), 1)
    adjacent[...] = jnp.where(jnp.abs(i - j) == 1, 1.0, 0.0).astype(jnp.bfloat16)

    greeted = jnp.where(has_x[0], 1, 0) + jnp.where(has_x[1], 1, 0) + devices_z - 1
    pl.semaphore_wait(barrier, greeted)

    def send_x(par, side, c, count=1):
        rows = pl.ds(pl.multiple_of(PAD + c * chunk, 8), count * chunk)
        mine, theirs = ((1, last + 1), (last, 0))[side]
        return pltpu.make_async_remote_copy(
            src_ref=buffers[par].at[:, :, mine, rows, :],
            dst_ref=buffers[par].at[:, :, theirs, rows, :],
            send_sem=xs_sem.at[par, side],
            recv_sem=xr_sem.at[par, side, c],
            device_id={"tx": to_x[side]},
            device_id_type=MESH,
        )

    def send_z(par, side, group, first, count):
        mine, theirs = ((PAD, PAD + depth), (PAD + depth - 1, PAD - 1))[side]
        return pltpu.make_async_remote_copy(
            src_ref=buffers[par].at[:, :, pl.ds(first, count), pl.ds(mine, 1), :],
            dst_ref=buffers[par].at[:, :, pl.ds(first, count), pl.ds(theirs, 1), :],
            send_sem=zs_sem.at[par, side],
            recv_sem=zr_sem.at[par, side, group],
            device_id={"dz": to_z[side]},
            device_id_type=MESH,
        )

    def when(condition, action):
        pl.when(condition)(action)

    def start_x(par, side, c, also=True):
        when(jnp.logical_and(has_x[side], also), lambda: send_x(par, side, c).start())

    def sent_x(par, side, also=True):
        when(jnp.logical_and(has_x[side], also), lambda: send_x(par, side, 0, CHUNKS).wait_send())

    def start_z(par, side, group, also=True):
        def start():
            for first, count in GROUPS[group]:
                send_z(par, side, group, first, count).start()

        when(jnp.logical_and(has_z[side], also), start)

    def sent_z(par, side, also=True):
        when(jnp.logical_and(has_z[side], also), lambda: send_z(par, side, 0, 1, planes).wait_send())

    def arrived_z(par, side, group, also=True):
        count = sum(count for _, count in GROUPS[group])
        when(jnp.logical_and(has_z[side], also), lambda: send_z(par, 1 - side, group, 1, count).wait_recv())

    def both(action, *args):
        for side in range(2):
            action(args[0], side, *args[1:])

    def start_first_z(side, group):
        row, theirs = ((0, PAD + depth), (depth - 1, PAD - 1))[side]

        def start():
            for first, count in GROUPS[group]:
                for f, r in fields:
                    for s in range(2):
                        pltpu.make_async_remote_copy(
                            src_ref=r.at[pl.ds(first - 1, count), pl.ds(row, 1), pl.ds(128 * s, 128)],
                            dst_ref=even.at[f, s, pl.ds(first, count), pl.ds(theirs, 1), :],
                            send_sem=zs_sem.at[0, side],
                            recv_sem=zr_sem.at[0, side, group],
                            device_id={"dz": to_z[side]},
                            device_id_type=MESH,
                        ).start()

        when(has_z[side], start)

    landed(0, even.at[:, :, pl.ds(1, 2), pl.ds(PAD, depth), :])
    for c in range(CHUNKS):
        both(start_x, 0, c)
        for side in range(2):
            start_first_z(side, (LOWER, EDGES, UPPER, BESIDE)[c])
    landed(1, even.at[:, :, pl.ds(1, planes - 2), pl.ds(PAD, depth), :])
    landed(2, rate)

    def edge(step, new, c):
        old = 1 - new
        ahead = step < STEPS
        arrived_z(old, 0, EDGES, c == 0)
        arrived_z(old, 1, EDGES, c == CHUNKS - 1)
        for side, x in ((0, 1), (1, last)):
            when(has_x[side], lambda: send_x(old, 1 - side, c).wait_recv())
            sent_x(new, side, jnp.logical_and(c == 0, step >= 2))
            advance(buffers[old], buffers[new], rate, adjacent, x, pl.multiple_of(c * chunk, chunk), chunk, False)
            start_x(new, side, c, ahead)
        start_z(new, 0, EDGES, c == 0)
        start_z(new, 1, EDGES, jnp.logical_and(c == CHUNKS - 1, ahead))

    def interior(new, low, high, stride=1):
        def plane(i, carry):
            advance(buffers[1 - new], buffers[new], rate, adjacent, low + i * stride, 0, depth, True)
            return carry

        lax.fori_loop(0, (high - low + stride - 1) // stride, plane, 0)

    def ahead_of(step, new, c):
        old = 1 - new
        if not isinstance(c, int):
            pl.when(c == 2)(lambda: both(arrived_z, old, UPPER))
            interior(new, 4 * c + 1, 4 * c + 5)

            @pl.when(c == 1)
            def _():
                start_z(new, 0, LOWER)
                start_z(new, 1, LOWER, step + 1 < STEPS)

        elif c == 0:
            both(arrived_z, old, LOWER)
            both(sent_z, new)
            interior(new, 3, 5)
        else:
            interior(new, 13, 15)
            start_z(new, 0, UPPER)
            start_z(new, 1, UPPER, step + 1 < STEPS)

    def send_colors(by, source, target, send_sem, recv_sem):
        peer = lax.rem(dz + by, devices_z)
        return pltpu.make_async_remote_copy(
            src_ref=source.at[peer // (devices_z // 2)],
            dst_ref=target.at[dz],
            send_sem=send_sem.at[0],
            recv_sem=recv_sem.at[0],
            device_id={"dz": peer},
            device_id_type=MESH,
        )

    def share_colors(source, target, send_sem, recv_sem):
        for by in sorted(range(1, devices_z), key=lambda by: abs(by - devices_z // 2)):
            send_colors(by, source, target, send_sem, recv_sem).start()
        target[dz] = source[dz // (devices_z // 2)]

    def shared_colors(source, target, send_sem, recv_sem):
        all_peers = target.at[pl.ds(0, devices_z - 1)]
        pltpu.make_async_copy(all_peers, all_peers, recv_sem.at[0]).wait()
        pltpu.make_async_copy(all_peers, all_peers, send_sem.at[0]).wait()

    inner_way = (colors, all_colors, cs_sem, cr_sem)
    edge_way = (edge_colors, all_edges, es_sem, er_sem)

    def render(low, high, stride=1):
        def plane(i, carry):
            x = low + i * stride
            for s, channels in enumerate(march(even, (x,), depth, thickness)):
                for ch, value in enumerate(channels):
                    colors[s, ch, pl.ds(x - 1, 1), :] = value
            return carry

        lax.fori_loop(0, (high - low + stride - 1) // stride, plane, 0)

    both(arrived_z, 0, LOWER)
    interior(1, 3, 9)
    both(start_z, 1, LOWER)

    def pair(it, carry):
        for new in (1, 0):
            step = 2 * it + (1 if new else 2)
            final = step == STEPS
            ahead = step < STEPS
            old = 1 - new

            edge(step, new, 0)
            if new:

                @pl.when(it == 0)
                def _():
                    both(arrived_z, 0, UPPER)
                    interior(1, 9, 15)
                    both(start_z, 1, UPPER)

            both(arrived_z, old, BESIDE)
            interior(new, 2, 16, 13)
            start_z(new, 0, BESIDE)
            start_z(new, 1, BESIDE, ahead)
            if new:
                ahead_of(step, 0, 0)
            else:
                pl.when(ahead)(lambda: ahead_of(step, 1, 0))

                @pl.when(final)
                def _():
                    arrived_z(0, 1, UPPER)
                    render(9, 13)

            def middle(c, carry, new=new, step=step, final=final, ahead=ahead):
                edge(step, new, c)
                if new:
                    ahead_of(step, 0, c)

                    @pl.when(jnp.logical_and(it == 1, c == 2))
                    def _():
                        arrived_z(0, 1, LOWER)
                        render(3, 5)

                else:
                    pl.when(ahead)(lambda: ahead_of(step, 1, c))

                    @pl.when(jnp.logical_and(final, c == 1))
                    def _():
                        render(13, 15)
                        arrived_z(0, 1, BESIDE)
                        render(2, 16, 13)
                        share_colors(*inner_way)

                return carry

            lax.fori_loop(1, 3, middle, 0)

            if new:
                edge(step, new, 3)
                ahead_of(step, 0, 3)
                pl.when(it == 1)(lambda: render(5, 9))
            else:

                @pl.when(ahead)
                def _():
                    edge(step, 0, 3)
                    ahead_of(step, 1, 3)

        return carry

    lax.fori_loop(0, STEPS // 2, pair, 0)

    arrived_z(1, 1, EDGES)
    arrived_z(0, 1, EDGES)
    later = jnp.where(lax.rem(tx, 4) == 0, 0, 1)

    def last_edge(k, carry):
        side = jnp.where(k == 0, 1 - later, later)
        x = jnp.where(side == 0, 1, last)
        rows = pl.ds(PAD + depth - chunk, chunk)
        inward = pltpu.make_async_copy(odd.at[:, :, x, rows, :], odd.at[:, :, x, rows, :], xr_sem.at[1, 1 - side, CHUNKS - 1])
        when(jnp.where(side == 0, tx > 0, tx < devices_x - 1), lambda: inward.wait())
        advance(odd, even, rate, adjacent, x, depth - chunk, chunk, False)
        for s, channels in enumerate(march(even, (x,), depth, thickness)):
            for ch, value in enumerate(channels):
                edge_colors[s, pl.ds(2 * ch + side, 1), :] = value
        return carry

    lax.fori_loop(0, 2, last_edge, 0)
    share_colors(*edge_way)

    both(sent_x, 1)
    both(sent_z, 1)
    sent_z(0, 0)
    shared_colors(*inner_way)
    shared_colors(*edge_way)


def results(state, all_colors, all_edges, image_out, fuel_out, heat_out, image_ref, sem, image_sem):
    devices_z, _, planes, _ = all_colors.shape
    depth = fuel_out.shape[1]
    share = image_ref.shape[2]
    dz = lax.axis_index("dz")
    piece = planes // 4
    for first in range(0, planes, piece):
        for f, target in ((0, fuel_out), (1, heat_out)):
            for s in range(2):
                pltpu.make_async_copy(
                    state.at[f, s, pl.ds(1 + first, piece), pl.ds(PAD, depth), :],
                    target.at[pl.ds(first, piece), :, pl.ds(128 * s, 128)],
                    sem.at[f],
                ).start()
    shift = lax.rem(128 - share * lax.rem(dz, devices_z // 2), 128)
    image = compose([[all_colors[b, ch] for ch in range(4)] for b in range(devices_z)])
    for ch in range(4):
        image_ref[ch] = pltpu.roll(image[ch], shift, 1)[:, :share]
    image = compose([[all_edges[b, 2 * ch : 2 * ch + 2, :] for ch in range(4)] for b in range(devices_z)])
    for ch in range(4):
        value = pltpu.roll(image[ch], shift, 1)[:, :share]
        image_ref[ch, 0:1] = value[0:1]
        image_ref[ch, planes - 1 : planes] = value[1:2]
    shown = pltpu.make_async_copy(image_ref, image_out, image_sem)
    shown.start()
    shown.wait()
    for f, target in ((0, fuel_out), (1, heat_out)):
        pltpu.make_async_copy(target, target, sem.at[f]).wait()


def body(fuel, heat, rate):
    planes, depth, width = fuel.shape
    devices_x, devices_z = lax.axis_size("tx"), lax.axis_size("dz")
    sizes = (devices_x, devices_z, planes, depth, width)
    anywhere = pl.BlockSpec(memory_space=pltpu.HBM)
    local = pl.BlockSpec(memory_space=pltpu.VMEM)
    block = pltpu.VMEM((2, 2, planes + 2, depth + ROWS_AFTER, 128), jnp.float32)
    dma = pltpu.SemaphoreType.DMA
    arrived = pl.pallas_call(
        functools.partial(kernel, sizes),
        out_shape=(
            block,
            pltpu.VMEM((devices_z, 4, planes, 128), jnp.float32),
            pltpu.VMEM((devices_z, 8, 128), jnp.float32),
        ),
        in_specs=[anywhere] * 3,
        out_specs=(local,) * 3,
        scratch_shapes=[
            block,
            pltpu.VMEM((2, planes, depth, 128), jnp.float32),
            pltpu.VMEM((width, width), jnp.bfloat16),
            pltpu.VMEM((2, 4, planes, 128), jnp.float32),
            pltpu.VMEM((2, 8, 128), jnp.float32),
            dma((3,)),
            dma((2, 2)),
            dma((2, 2, CHUNKS)),
            dma((2, 2)),
            dma((2, 2, len(GROUPS))),
            dma((1,)),
            dma((1,)),
            dma((1,)),
            dma((1,)),
        ],
        compiler_params=pltpu.CompilerParams(
            collective_id=0, has_side_effects=True, vmem_limit_bytes=40 * 2**20
        ),
    )(*(pltpu.with_memory_space_constraint(a, pltpu.HBM) for a in (fuel, heat, rate)))
    return pl.pallas_call(
        results,
        out_shape=(
            jax.ShapeDtypeStruct((4, planes, width // devices_z), jnp.float32),
            jax.ShapeDtypeStruct(fuel.shape, jnp.float32),
            jax.ShapeDtypeStruct(fuel.shape, jnp.float32),
        ),
        in_specs=[local] * 3,
        out_specs=(anywhere,) * 3,
        scratch_shapes=[
            pltpu.VMEM((4, planes, width // devices_z), jnp.float32),
            dma((2,)),
            dma,
        ],
        compiler_params=pltpu.CompilerParams(vmem_limit_bytes=40 * 2**20),
    )(*arrived)


def solution(mesh):
    placed = (P("tx", "dz", None),) * 3
    return jax.shard_map(
        body,
        mesh=mesh,
        in_specs=placed,
        out_specs=(P(None, "tx", "dz"), P("tx", "dz", None), P("tx", "dz", None)),
        check_vma=False,
    )
```

```python
import functools

import jax
import jax.numpy as jnp
from jax import lax
from jax.experimental import pallas as pl
from jax.experimental.pallas import tpu as pltpu
from jax.sharding import PartitionSpec as P

STEPS = 4
FUEL_SPREAD = 0.15
HEAT_SPREAD = 0.12
ACTIVATION = 1.5
RELEASE = 2.0
OPACITY = 1.5
LOG2E = 1.4426950408889634
MESH = pl.DeviceIdType.MESH

PAD = 8
ROWS_AFTER = 24
CHUNKS = 4
SEGMENTS = 8
GROUPS = (((2, 1), (15, 1)), ((3, 6),), ((9, 4),), ((13, 2),), ((1, 1), (16, 1)), ((1, 1), (16, 1)))
BESIDE, LOWER, UPPER, LAST, EDGES = range(5)
PAIRS = ((1, 16), (2, 15), (13, 14))


def split(value):
    high = value.astype(jnp.bfloat16)
    low = (value - high.astype(jnp.float32)).astype(jnp.bfloat16)
    return high, low


def step_of(src, dst, rate, x, start, rows, halves, center, across):
    here = pl.ds(start + PAD, rows)
    mixed = []
    for f, spread in ((0, FUEL_SPREAD), (1, HEAT_SPREAD)):
        row = []
        for k, s in enumerate(halves):
            view = src.at[f, s, x, pl.ds(start, rows + 2 * PAD), :]
            beside = view[PAD - 1 : PAD - 1 + rows] + view[PAD + 1 : PAD + 1 + rows]
            beside = beside + (src[f, s, x - 1, here, :] + src[f, s, x + 1, here, :])
            beside = beside + across[f][k]
            row.append((1.0 - 6.0 * spread) * center[f][k] + spread * beside)
        mixed.append(row)
    for k, s in enumerate(halves):
        fuel, heat = mixed[0][k], mixed[1][k]
        inverse = pl.reciprocal(1.0 + heat, approx=False)
        speed = jnp.exp2(ACTIVATION * LOG2E - (ACTIVATION * LOG2E) * inverse)
        burned = rate[s, x - 1, pl.ds(start, rows), :] * fuel * speed
        dst[0, s, x, here, :] = fuel - burned
        dst[1, s, x, here, :] = heat + RELEASE * burned


def advance(src, dst, rate, adjacent, x, rows):
    center = [[src[f, s, x, pl.ds(PAD, rows), :] for s in range(2)] for f in range(2)]
    parts = [split(jnp.concatenate(center[f], axis=1)) for f in range(2)]
    sums = jnp.dot(
        jnp.concatenate([*parts[0], *parts[1]], axis=0),
        adjacent[...],
        preferred_element_type=jnp.float32,
    )
    across = []
    for f in range(2):
        total = sums[2 * f * rows : (2 * f + 1) * rows] + sums[(2 * f + 1) * rows : (2 * f + 2) * rows]
        across.append((total[:, :128], total[:, 128:]))
    step_of(src, dst, rate, x, 0, rows, range(2), center, across)


def advance_half(src, dst, rate, x, s, start, rows):
    here = pl.ds(start + PAD, rows)
    center = [[src[f, s, x, here, :]] for f in range(2)]
    lane = lax.broadcasted_iota(jnp.int32, (rows, 128), 1)
    seam = jnp.where(s == 0, 127, 0)
    shift = jnp.where(s == 0, 127, 1)
    across = []
    for f in range(2):
        mine = center[f][0]
        total = jnp.where(lane == 0, 0.0, pltpu.roll(mine, 1, 1)) + jnp.where(lane == 127, 0.0, pltpu.roll(mine, 127, 1))
        other = pltpu.roll(src[f, 1 - s, x, here, :], shift, 1)
        across.append([total + jnp.where(lane == seam, other, 0.0)])
    step_of(src, dst, rate, x, start, rows, [s], center, across)


def march(state, x, s, depth, thickness):
    length = depth // SEGMENTS + 1
    full = depth - (SEGMENTS - 1) * length
    rate = -0.5 * thickness * LOG2E
    sub = lax.broadcasted_iota(jnp.int32, (SEGMENTS, 128), 0)
    zero = jnp.zeros((SEGMENTS, 128), jnp.float32)
    rows = lambda f, v: state[f, s, x, pl.ds(PAD + v, SEGMENTS, stride=length), :]
    red, green, blue, passed = zero, zero, zero, zero
    through = zero + 1.0
    fuel, heat = rows(0, 0), rows(1, 0)
    for v in range(length):
        next_fuel, next_heat = rows(0, v + 1), rows(1, v + 1)
        both_fuel, both_heat = fuel + next_fuel, heat + next_heat
        if v >= full:
            both_fuel = jnp.where(sub < SEGMENTS - 1, both_fuel, 0.0)
            both_heat = jnp.where(sub < SEGMENTS - 1, both_heat, 0.0)
        passed = passed + both_heat
        later = jnp.exp2(rate * passed)
        weight = through - later
        glow = 1.0 - 2.0 * pl.reciprocal(2.0 + both_heat, approx=False)
        shaded = weight * both_fuel
        red = red + weight * glow
        green = green + shaded
        blue = blue + shaded * glow
        through, fuel, heat = later, next_fuel, next_heat
    before = passed
    for by in (1, 2, 4):
        before = before + jnp.where(sub >= by, pltpu.roll(before, by, 0), 0.0)
    share = jnp.exp2(rate * (before - passed))
    return [
        jnp.sum(share * red, axis=0, keepdims=True),
        0.5 * jnp.sum(share * green, axis=0, keepdims=True),
        0.5 * jnp.sum(share * blue, axis=0, keepdims=True),
        (0.5 * thickness) * jnp.sum(passed, axis=0, keepdims=True),
    ]


def compose(pieces):
    before = jnp.zeros_like(pieces[0][3])
    total = [jnp.zeros_like(before) for _ in range(3)]
    for piece in pieces:
        share = jnp.exp2(-LOG2E * before)
        total = [t + share * c for t, c in zip(total, piece[:3])]
        before = before + piece[3]
    return total + [1.0 - jnp.exp2(-LOG2E * before)]


def kernel(
    sizes,
    fuel_ref,
    heat_ref,
    rate_ref,
    even,
    all_colors,
    all_edges,
    odd,
    rate,
    adjacent,
    colors,
    edge_colors,
    in_sem,
    xs_sem,
    xr_sem,
    zs_sem,
    zr_sem,
    cs_sem,
    cr_sem,
    es_sem,
    er_sem,
):
    devices_x, devices_z, planes, depth, width = sizes
    tx, dz = lax.axis_index("tx"), lax.axis_index("dz")
    thickness = OPACITY / (depth * devices_z)
    buffers = (even, odd)
    chunk = 2 * depth // CHUNKS
    mine = dz // (devices_z // 2)
    last = planes
    has_x = (tx > 0, tx < devices_x - 1)
    has_z = (dz > 0, dz < devices_z - 1)
    to_x = (tx - 1, tx + 1)
    to_z = (dz - 1, dz + 1)

    barrier = pltpu.get_barrier_semaphore()
    for side in range(2):

        @pl.when(has_x[side])
        def _():
            pl.semaphore_signal(barrier, inc=1, device_id={"tx": to_x[side]}, device_id_type=MESH)

    for by in range(1, devices_z):
        peer = lax.rem(dz + by, devices_z)
        pl.semaphore_signal(barrier, inc=1, device_id={"dz": peer}, device_id_type=MESH)

    def load(source, target, k, first, count, at, s):
        return pltpu.make_async_copy(
            source.at[pl.ds(first, count), :, pl.ds(128 * s, 128)], target.at[s, pl.ds(first + at, count)], in_sem.at[k]
        )

    even_rows = [even.at[f, :, :, pl.ds(PAD, depth), :] for f in range(2)]
    fields = ((0, fuel_ref), (1, heat_ref))
    edges = [load(r, even_rows[f], 0, x, 1, 1, s) for x in (0, planes - 1) for f, r in fields for s in range(2)]
    inner = [load(r, even_rows[f], 1, 1, planes - 2, 1, s) for f, r in fields for s in range(2)]
    rates = [load(rate_ref, rate, 2, 0, planes, 0, s) for s in range(2)]

    def landed(k, block):
        pltpu.make_async_copy(block, block, in_sem.at[k]).wait()

    for copy in edges + inner + rates:
        copy.start()

    for side, plane in ((0, 0), (1, last + 1)):

        @pl.when(jnp.logical_not(has_x[side]))
        def _():
            def clear(r, carry):
                for buffer in buffers:
                    for f in range(2):
                        for s in range(2):
                            rows = pl.ds(PAD + r * chunk, chunk)
                            buffer[f, s, plane, rows, :] = jnp.zeros((chunk, 128), jnp.float32)
                return carry

            lax.fori_loop(0, CHUNKS // 2, clear, 0)

    for side, at in ((0, 0), (1, PAD + depth)):

        @pl.when(jnp.logical_not(has_z[side]))
        def _():
            def clear(x, carry):
                for buffer in buffers:
                    for f in range(2):
                        for s in range(2):
                            buffer[f, s, x, at : at + PAD, :] = jnp.zeros((PAD, 128), jnp.float32)
                return carry

            lax.fori_loop(1, last + 1, clear, 0)

    i = lax.broadcasted_iota(jnp.int32, (width, width), 0)
    j = lax.broadcasted_iota(jnp.int32, (width, width), 1)
    adjacent[...] = jnp.where(jnp.abs(i - j) == 1, 1.0, 0.0).astype(jnp.bfloat16)

    greeted = jnp.where(has_x[0], 1, 0) + jnp.where(has_x[1], 1, 0) + devices_z - 1
    pl.semaphore_wait(barrier, greeted)

    def piece(c):
        return jnp.where(c % 2 == 0, 1 - mine, mine), (c // 2) * chunk

    def send_x(par, side, c=None):
        if c is None:
            part = (slice(None), pl.ds(PAD, depth))
        else:
            half, start = piece(c)
            part = (half, pl.ds(pl.multiple_of(PAD + start, 8), chunk))
        ours, theirs = ((1, last + 1), (last, 0))[side]
        return pltpu.make_async_remote_copy(
            src_ref=buffers[par].at[:, part[0], ours, part[1], :],
            dst_ref=buffers[par].at[:, part[0], theirs, part[1], :],
            send_sem=xs_sem.at[par, side],
            recv_sem=xr_sem.at[par, side, 0 if c is None else c],
            device_id={"tx": to_x[side]},
            device_id_type=MESH,
        )

    def send_z(par, side, group, first, count, halves=slice(None)):
        ours, theirs = ((PAD, PAD + depth), (PAD + depth - 1, PAD - 1))[side]
        return pltpu.make_async_remote_copy(
            src_ref=buffers[par].at[:, halves, pl.ds(first, count), pl.ds(ours, 1), :],
            dst_ref=buffers[par].at[:, halves, pl.ds(first, count), pl.ds(theirs, 1), :],
            send_sem=zs_sem.at[par, side],
            recv_sem=zr_sem.at[par, side, group],
            device_id={"dz": to_z[side]},
            device_id_type=MESH,
        )

    def when(condition, action):
        pl.when(condition)(action)

    def start_x(par, side, c, also=True):
        when(jnp.logical_and(has_x[side], also), lambda: send_x(par, side, c).start())

    def sent_x(par, side, also=True):
        when(jnp.logical_and(has_x[side], also), lambda: send_x(par, side).wait_send())

    def start_z(par, side, group, also=True):
        def start():
            for first, count in GROUPS[group]:
                send_z(par, side, group, first, count).start()

        when(jnp.logical_and(has_z[side], also), start)

    def sent_z(par, side, also=True):
        when(jnp.logical_and(has_z[side], also), lambda: send_z(par, side, 0, 1, planes).wait_send())

    def arrived_z(par, side, group, also=True):
        count = sum(count for _, count in GROUPS[group])
        when(jnp.logical_and(has_z[side], also), lambda: send_z(par, 1 - side, group, 1, count).wait_recv())

    def start_edge_z(par, side, half, also=True):
        def start():
            for x in (1, last):
                send_z(par, side, EDGES + half, x, 1, half).start()

        when(jnp.logical_and(has_z[side], also), start)

    def arrived_edge_z(par, side, half, also=True):
        when(jnp.logical_and(has_z[side], also), lambda: send_z(par, 1 - side, EDGES + half, 1, 2, half).wait_recv())

    def both(action, *args):
        for side in range(2):
            action(args[0], side, *args[1:])

    def start_first_z(side, group):
        row, theirs = ((0, PAD + depth), (depth - 1, PAD - 1))[side]

        def start():
            for first, count in GROUPS[group]:
                for f, r in fields:
                    for s in range(2):
                        pltpu.make_async_remote_copy(
                            src_ref=r.at[pl.ds(first - 1, count), pl.ds(row, 1), pl.ds(128 * s, 128)],
                            dst_ref=even.at[f, s, pl.ds(first, count), pl.ds(theirs, 1), :],
                            send_sem=zs_sem.at[0, side],
                            recv_sem=zr_sem.at[0, side, group + (s if group == EDGES else 0)],
                            device_id={"dz": to_z[side]},
                            device_id_type=MESH,
                        ).start()

        when(has_z[side], start)

    landed(0, even.at[:, :, pl.ds(1, 2), pl.ds(PAD, depth), :])
    for c in range(CHUNKS):
        both(start_x, 0, c)
        for side in range(2):
            for group in ((LOWER,), (EDGES,), (UPPER, LAST), (BESIDE,))[c]:
                start_first_z(side, group)
    landed(1, even.at[:, :, pl.ds(1, planes - 2), pl.ds(PAD, depth), :])
    landed(2, rate)

    def edge(step, new, c):
        old = 1 - new
        ahead = step < STEPS
        half, start = piece(c)
        below, above = c < CHUNKS // 2, c >= CHUNKS // 2
        arrived_edge_z(old, 0, half, below)
        arrived_edge_z(old, 1, half, above)
        for side, x in ((0, 1), (1, last)):
            when(has_x[side], lambda: send_x(old, 1 - side, c).wait_recv())
            sent_x(new, side, jnp.logical_and(c == 0, step >= 2))
            advance_half(buffers[old], buffers[new], rate, x, half, pl.multiple_of(start, chunk), chunk)
            start_x(new, side, c, ahead)
        start_edge_z(new, 0, half, below)
        start_edge_z(new, 1, half, jnp.logical_and(above, ahead))

    def interior(new, low, high, stride=1):
        def plane(i, carry):
            advance(buffers[1 - new], buffers[new], rate, adjacent, low + i * stride, depth)
            return carry

        lax.fori_loop(0, (high - low + stride - 1) // stride, plane, 0)

    def ahead_of(step, new, c):
        old = 1 - new
        if not isinstance(c, int):
            pl.when(c == 2)(lambda: both(arrived_z, old, UPPER))
            interior(new, 4 * c + 1, 4 * c + 5)
            for at, group in ((1, LOWER), (2, UPPER)):
                start_z(new, 0, group, c == at)
                start_z(new, 1, group, jnp.logical_and(c == at, step + 1 < STEPS))

        elif c == 0:
            both(arrived_z, old, LOWER)
            both(sent_z, new)
            interior(new, 3, 5)
        else:
            both(arrived_z, old, LAST)
            interior(new, 13, 15)
            start_z(new, 0, LAST)
            start_z(new, 1, LAST, step + 1 < STEPS)

    def send_colors(peer, source, target, send_sem, recv_sem):
        return pltpu.make_async_remote_copy(
            src_ref=source(peer // (devices_z // 2)),
            dst_ref=target(dz),
            send_sem=send_sem,
            recv_sem=recv_sem,
            device_id={"dz": peer},
            device_id_type=MESH,
        )

    group = devices_z // 2
    far = [(1 - mine) * group + lax.rem(dz + by, group) for by in range(group)]
    near = [mine * group + lax.rem(dz + by, group) for by in range(1, group)]

    def shared_colors(count, target, send_sem, recv_sem):
        all_peers = target(pl.ds(0, count))
        pltpu.make_async_copy(all_peers, all_peers, recv_sem).wait()
        pltpu.make_async_copy(all_peers, all_peers, send_sem).wait()

    edge_halves, edge_peers = lambda half: edge_colors.at[0, half], lambda peers: all_edges.at[0, peers]
    inner_way = (lambda half: colors.at[half], lambda peers: all_colors.at[peers], cs_sem.at[0], cr_sem.at[0])
    far_way = (edge_halves, edge_peers, es_sem.at[0], er_sem.at[0])
    near_way = (edge_halves, edge_peers, es_sem.at[1], er_sem.at[1])
    pairs = pl.ds(1, len(PAIRS) - 1)
    pairs_way = (
        lambda half: edge_colors.at[pairs, half],
        lambda peers: all_edges.at[pairs, peers],
        es_sem.at[2],
        er_sem.at[2],
    )

    def render_pair(pair, side, half):
        x = jnp.where(side == 0, *PAIRS[pair])
        for ch, value in enumerate(march(even, x, half, depth, thickness)):
            edge_colors[pair, half, pl.ds(2 * ch + side, 1), :] = value

    def render(low, high, stride=1):
        def plane(i, carry):
            x = low + i * stride
            for s in range(2):
                for ch, value in enumerate(march(even, x, s, depth, thickness)):
                    colors[s, ch, pl.ds(x - 1, 1), :] = value
            return carry

        lax.fori_loop(0, (high - low + stride - 1) // stride, plane, 0)

    both(arrived_z, 0, LOWER)
    interior(1, 3, 9)
    both(start_z, 1, LOWER)

    def pair(it, carry):
        for new in (1, 0):
            step = 2 * it + (1 if new else 2)
            final = step == STEPS
            ahead = step < STEPS
            old = 1 - new

            edge(step, new, 0)
            if new:

                @pl.when(it == 0)
                def _():
                    both(arrived_z, 0, UPPER)
                    both(arrived_z, 0, LAST)
                    interior(1, 9, 15)
                    both(start_z, 1, UPPER)
                    both(start_z, 1, LAST)

            both(arrived_z, old, BESIDE)
            interior(new, 2, 16, 13)
            start_z(new, 0, BESIDE)
            start_z(new, 1, BESIDE, ahead)
            if new:
                ahead_of(step, 0, 0)
            else:
                pl.when(ahead)(lambda: ahead_of(step, 1, 0))

                @pl.when(final)
                def _():
                    arrived_z(0, 1, UPPER)
                    render(9, 13)
                    for peer in far + near:
                        send_colors(peer, *inner_way).start()
                    all_colors[dz] = colors[mine]

            def middle(c, carry, new=new, step=step, final=final, ahead=ahead):
                edge(step, new, c)
                if new:
                    ahead_of(step, 0, c)

                    @pl.when(jnp.logical_and(it == 1, c == 2))
                    def _():
                        arrived_z(0, 1, LOWER)
                        render(3, 5)

                else:
                    pl.when(ahead)(lambda: ahead_of(step, 1, c))

                    @pl.when(jnp.logical_and(final, c == 1))
                    def _():
                        arrived_z(0, 1, LAST)
                        arrived_z(0, 1, BESIDE)

                        def sides(side, carry):
                            for pair in range(1, len(PAIRS)):
                                for half in range(2):
                                    render_pair(pair, side, half)
                            return carry

                        lax.fori_loop(0, 2, sides, 0)
                        for peer in far + near:
                            send_colors(peer, *pairs_way).start()
                        all_edges[pairs, dz] = edge_colors[pairs, mine]

                    @pl.when(jnp.logical_and(final, c == 2))
                    def _():
                        arrived_edge_z(0, 1, 1 - mine)
                        lax.fori_loop(0, 2, lambda side, _: render_pair(0, side, 1 - mine), None)
                        for peer in far:
                            send_colors(peer, *far_way).start()

                return carry

            lax.fori_loop(1, 3, middle, 0)

            if new:
                edge(step, new, 3)
                ahead_of(step, 0, 3)
                pl.when(it == 1)(lambda: render(5, 9))
            else:

                @pl.when(ahead)
                def _():
                    edge(step, 0, 3)
                    ahead_of(step, 1, 3)

        return carry

    lax.fori_loop(0, STEPS // 2, pair, 0)

    arrived_edge_z(1, 1, mine)
    arrived_edge_z(0, 1, mine)
    later = jnp.where(lax.rem(tx, 4) == 0, 0, 1)

    def last_edge(k, carry):
        side = jnp.where(k == 0, 1 - later, later)
        x = jnp.where(side == 0, 1, last)
        block = odd.at[:, mine, x, pl.ds(PAD + depth - chunk, chunk), :]
        inward = pltpu.make_async_copy(block, block, xr_sem.at[1, 1 - side, CHUNKS - 1])
        when(jnp.where(side == 0, tx > 0, tx < devices_x - 1), lambda: inward.wait())
        advance_half(odd, even, rate, x, mine, depth - chunk, chunk)
        render_pair(0, side, mine)
        return carry

    lax.fori_loop(0, 2, last_edge, 0)
    for peer in near:
        send_colors(peer, *near_way).start()
    all_edges[0, dz] = edge_colors[0, mine]

    both(sent_x, 1)
    both(sent_z, 1)
    sent_z(0, 0)
    shared_colors(devices_z - 1, *inner_way[1:])
    shared_colors(devices_z - 1, *pairs_way[1:])
    shared_colors(group, *far_way[1:])
    shared_colors(group - 1, *near_way[1:])


def results(state, all_colors, all_edges, image_out, fuel_out, heat_out, image_ref, sem, image_sem):
    devices_z, _, planes, _ = all_colors.shape
    depth = fuel_out.shape[1]
    share = image_ref.shape[2]
    dz = lax.axis_index("dz")
    piece = planes // 4
    for first in range(0, planes, piece):
        for f, target in ((0, fuel_out), (1, heat_out)):
            for s in range(2):
                pltpu.make_async_copy(
                    state.at[f, s, pl.ds(1 + first, piece), pl.ds(PAD, depth), :],
                    target.at[pl.ds(first, piece), :, pl.ds(128 * s, 128)],
                    sem.at[f],
                ).start()
    shift = lax.rem(128 - share * lax.rem(dz, devices_z // 2), 128)
    image = compose([[all_colors[b, ch] for ch in range(4)] for b in range(devices_z)])
    for ch in range(4):
        image_ref[ch] = pltpu.roll(image[ch], shift, 1)[:, :share]
    for pair, planes_of in enumerate(PAIRS):
        rows = [[all_edges[pair, b, 2 * ch : 2 * ch + 2, :] for ch in range(4)] for b in range(devices_z)]
        image = compose(rows)
        for ch in range(4):
            value = pltpu.roll(image[ch], shift, 1)[:, :share]
            for side, x in enumerate(planes_of):
                image_ref[ch, x - 1 : x] = value[side : side + 1]
    shown = pltpu.make_async_copy(image_ref, image_out, image_sem)
    shown.start()
    shown.wait()
    for f, target in ((0, fuel_out), (1, heat_out)):
        pltpu.make_async_copy(target, target, sem.at[f]).wait()


def body(fuel, heat, rate):
    planes, depth, width = fuel.shape
    devices_x, devices_z = lax.axis_size("tx"), lax.axis_size("dz")
    sizes = (devices_x, devices_z, planes, depth, width)
    anywhere = pl.BlockSpec(memory_space=pltpu.HBM)
    local = pl.BlockSpec(memory_space=pltpu.VMEM)
    block = pltpu.VMEM((2, 2, planes + 2, depth + ROWS_AFTER, 128), jnp.float32)
    dma = pltpu.SemaphoreType.DMA
    arrived = pl.pallas_call(
        functools.partial(kernel, sizes),
        out_shape=(
            block,
            pltpu.VMEM((devices_z, 4, planes, 128), jnp.float32),
            pltpu.VMEM((len(PAIRS), devices_z, 8, 128), jnp.float32),
        ),
        in_specs=[anywhere] * 3,
        out_specs=(local,) * 3,
        scratch_shapes=[
            block,
            pltpu.VMEM((2, planes, depth, 128), jnp.float32),
            pltpu.VMEM((width, width), jnp.bfloat16),
            pltpu.VMEM((2, 4, planes, 128), jnp.float32),
            pltpu.VMEM((len(PAIRS), 2, 8, 128), jnp.float32),
            dma((3,)),
            dma((2, 2)),
            dma((2, 2, CHUNKS)),
            dma((2, 2)),
            dma((2, 2, len(GROUPS))),
            dma((1,)),
            dma((1,)),
            dma((3,)),
            dma((3,)),
        ],
        compiler_params=pltpu.CompilerParams(
            collective_id=0, has_side_effects=True, vmem_limit_bytes=40 * 2**20
        ),
    )(*(pltpu.with_memory_space_constraint(a, pltpu.HBM) for a in (fuel, heat, rate)))
    return pl.pallas_call(
        results,
        out_shape=(
            jax.ShapeDtypeStruct((4, planes, width // devices_z), jnp.float32),
            jax.ShapeDtypeStruct(fuel.shape, jnp.float32),
            jax.ShapeDtypeStruct(fuel.shape, jnp.float32),
        ),
        in_specs=[local] * 3,
        out_specs=(anywhere,) * 3,
        scratch_shapes=[
            pltpu.VMEM((4, planes, width // devices_z), jnp.float32),
            dma((2,)),
            dma,
        ],
        compiler_params=pltpu.CompilerParams(vmem_limit_bytes=40 * 2**20),
    )(*arrived)


def solution(mesh):
    placed = (P("tx", "dz", None),) * 3
    return jax.shard_map(
        body,
        mesh=mesh,
        in_specs=placed,
        out_specs=(P(None, "tx", "dz"), P("tx", "dz", None), P("tx", "dz", None)),
        check_vma=False,
    )
```

```python
import functools

import jax
import jax.numpy as jnp
from jax import lax
from jax.experimental import pallas as pl
from jax.experimental.pallas import tpu as pltpu
from jax.sharding import PartitionSpec as P

STEPS = 4
FUEL_SPREAD = 0.15
HEAT_SPREAD = 0.12
ACTIVATION = 1.5
RELEASE = 2.0
OPACITY = 1.5
LOG2E = 1.4426950408889634
MESH = pl.DeviceIdType.MESH

PAD = 8
ROWS_AFTER = 56
CHUNKS = 4
SEGMENTS = 8
GROUPS = (((2, 1), (15, 1)), ((3, 6),), ((9, 4),), ((13, 2),), ((1, 1), (16, 1)))
BESIDE, LOWER, UPPER, LAST, EDGES = range(5)
PAIRS = ((1, 16), (2, 15), (13, 14))


def split(value):
    high = value.astype(jnp.bfloat16)
    low = (value - high.astype(jnp.float32)).astype(jnp.bfloat16)
    return high, low


def step_of(src, dst, rate, x, start, rows, halves, center, across):
    here = pl.ds(start + PAD, rows)
    mixed = []
    for f, spread in ((0, FUEL_SPREAD), (1, HEAT_SPREAD)):
        row = []
        for k, s in enumerate(halves):
            view = src.at[f, s, x, pl.ds(start, rows + 2 * PAD), :]
            beside = view[PAD - 1 : PAD - 1 + rows] + view[PAD + 1 : PAD + 1 + rows]
            beside = beside + (src[f, s, x - 1, here, :] + src[f, s, x + 1, here, :])
            beside = beside + across[f][k]
            row.append((1.0 - 6.0 * spread) * center[f][k] + spread * beside)
        mixed.append(row)
    for k, s in enumerate(halves):
        fuel, heat = mixed[0][k], mixed[1][k]
        inverse = pl.reciprocal(1.0 + heat, approx=False)
        speed = jnp.exp2(ACTIVATION * LOG2E - (ACTIVATION * LOG2E) * inverse)
        burned = rate[s, x - 1, pl.ds(start, rows), :] * fuel * speed
        dst[0, s, x, here, :] = fuel - burned
        dst[1, s, x, here, :] = heat + RELEASE * burned


def advance(src, dst, rate, adjacent, x, rows):
    center = [[src[f, s, x, pl.ds(PAD, rows), :] for s in range(2)] for f in range(2)]
    parts = [split(jnp.concatenate(center[f], axis=1)) for f in range(2)]
    sums = jnp.dot(
        jnp.concatenate([*parts[0], *parts[1]], axis=0),
        adjacent[...],
        preferred_element_type=jnp.float32,
    )
    across = []
    for f in range(2):
        total = sums[2 * f * rows : (2 * f + 1) * rows] + sums[(2 * f + 1) * rows : (2 * f + 2) * rows]
        across.append((total[:, :128], total[:, 128:]))
    step_of(src, dst, rate, x, 0, rows, range(2), center, across)


def advance_half(src, dst, rate, x, s, start, rows):
    here = pl.ds(start + PAD, rows)
    center = [[src[f, s, x, here, :]] for f in range(2)]
    lane = lax.broadcasted_iota(jnp.int32, (rows, 128), 1)
    seam = jnp.where(s == 0, 127, 0)
    shift = jnp.where(s == 0, 127, 1)
    across = []
    for f in range(2):
        mine = center[f][0]
        total = jnp.where(lane == 0, 0.0, pltpu.roll(mine, 1, 1)) + jnp.where(lane == 127, 0.0, pltpu.roll(mine, 127, 1))
        other = pltpu.roll(src[f, 1 - s, x, here, :], shift, 1)
        across.append([total + jnp.where(lane == seam, other, 0.0)])
    step_of(src, dst, rate, x, start, rows, [s], center, across)


def march(state, x, s, depth, thickness):
    length = depth // SEGMENTS + 1
    full = depth - (SEGMENTS - 1) * length
    rate = -0.5 * thickness * LOG2E
    sub = lax.broadcasted_iota(jnp.int32, (SEGMENTS, 128), 0)
    zero = jnp.zeros((SEGMENTS, 128), jnp.float32)
    rows = lambda f, v: state[f, s, x, pl.ds(PAD + v, SEGMENTS, stride=length), :]
    red, green, blue, passed = zero, zero, zero, zero
    through = zero + 1.0
    fuel, heat = rows(0, 0), rows(1, 0)
    for v in range(length):
        next_fuel, next_heat = rows(0, v + 1), rows(1, v + 1)
        both_fuel, both_heat = fuel + next_fuel, heat + next_heat
        if v >= full:
            both_fuel = jnp.where(sub < SEGMENTS - 1, both_fuel, 0.0)
            both_heat = jnp.where(sub < SEGMENTS - 1, both_heat, 0.0)
        passed = passed + both_heat
        later = jnp.exp2(rate * passed)
        weight = through - later
        glow = 1.0 - 2.0 * pl.reciprocal(2.0 + both_heat, approx=False)
        shaded = weight * both_fuel
        red = red + weight * glow
        green = green + shaded
        blue = blue + shaded * glow
        through, fuel, heat = later, next_fuel, next_heat
    before = passed
    for by in (1, 2, 4):
        before = before + jnp.where(sub >= by, pltpu.roll(before, by, 0), 0.0)
    share = jnp.exp2(rate * (before - passed))
    return [
        jnp.sum(share * red, axis=0, keepdims=True),
        0.5 * jnp.sum(share * green, axis=0, keepdims=True),
        0.5 * jnp.sum(share * blue, axis=0, keepdims=True),
        (0.5 * thickness) * jnp.sum(passed, axis=0, keepdims=True),
    ]


def compose(pieces):
    before = jnp.zeros_like(pieces[0][3])
    total = [jnp.zeros_like(before) for _ in range(3)]
    for piece in pieces:
        share = jnp.exp2(-LOG2E * before)
        total = [t + share * c for t, c in zip(total, piece[:3])]
        before = before + piece[3]
    return total + [1.0 - jnp.exp2(-LOG2E * before)]


def kernel(
    sizes,
    fuel_ref,
    heat_ref,
    rate_ref,
    even,
    all_colors,
    all_edges,
    odd,
    rate,
    adjacent,
    colors,
    edge_colors,
    in_sem,
    xs_sem,
    xr_sem,
    zs_sem,
    zr_sem,
    cs_sem,
    cr_sem,
    es_sem,
    er_sem,
    word_sem,
):
    devices_x, devices_z, planes, depth, width = sizes
    tx, dz = lax.axis_index("tx"), lax.axis_index("dz")
    thickness = OPACITY / (depth * devices_z)
    buffers = (even, odd)
    chunk = 2 * depth // CHUNKS
    mine = dz // (devices_z // 2)
    last = planes
    has_x = (tx > 0, tx < devices_x - 1)
    has_z = (dz > 0, dz < devices_z - 1)
    to_x = (tx - 1, tx + 1)
    to_z = (dz - 1, dz + 1)

    barrier = pltpu.get_barrier_semaphore()
    for side in range(2):

        @pl.when(has_x[side])
        def _():
            pl.semaphore_signal(barrier, inc=1, device_id={"tx": to_x[side]}, device_id_type=MESH)

    for side in range(2):

        @pl.when(has_z[side])
        def _():
            pl.semaphore_signal(barrier, inc=1, device_id={"dz": to_z[side]}, device_id_type=MESH)

    def load(source, target, k, first, count, at, s):
        return pltpu.make_async_copy(
            source.at[pl.ds(first, count), :, pl.ds(128 * s, 128)], target.at[s, pl.ds(first + at, count)], in_sem.at[k]
        )

    even_rows = [even.at[f, :, :, pl.ds(PAD, depth), :] for f in range(2)]
    fields = ((0, fuel_ref), (1, heat_ref))
    edges = [load(r, even_rows[f], 0, x, 1, 1, s) for x in (0, planes - 1) for f, r in fields for s in range(2)]
    inner = [load(r, even_rows[f], 1, 1, planes - 2, 1, s) for f, r in fields for s in range(2)]
    rates = [load(rate_ref, rate, 2, 0, planes, 0, s) for s in range(2)]

    def landed(k, block):
        pltpu.make_async_copy(block, block, in_sem.at[k]).wait()

    for copy in edges + inner + rates:
        copy.start()

    for side, plane in ((0, 0), (1, last + 1)):

        @pl.when(jnp.logical_not(has_x[side]))
        def _():
            def clear(r, carry):
                for buffer in buffers:
                    for f in range(2):
                        for s in range(2):
                            rows = pl.ds(PAD + r * chunk, chunk)
                            buffer[f, s, plane, rows, :] = jnp.zeros((chunk, 128), jnp.float32)
                return carry

            lax.fori_loop(0, CHUNKS // 2, clear, 0)

    for side, at in ((0, 0), (1, PAD + depth)):

        @pl.when(jnp.logical_not(has_z[side]))
        def _():
            def clear(x, carry):
                for buffer in buffers:
                    for f in range(2):
                        for s in range(2):
                            buffer[f, s, x, at : at + PAD, :] = jnp.zeros((PAD, 128), jnp.float32)
                return carry

            lax.fori_loop(1, last + 1, clear, 0)

    i = lax.broadcasted_iota(jnp.int32, (width, width), 0)
    j = lax.broadcasted_iota(jnp.int32, (width, width), 1)
    adjacent[...] = jnp.where(jnp.abs(i - j) == 1, 1.0, 0.0).astype(jnp.bfloat16)

    greeted = sum(jnp.where(near, 1, 0) for near in has_x + has_z)
    pl.semaphore_wait(barrier, greeted)

    def piece(c):
        return jnp.where(c % 2 == 0, 1 - mine, mine), (c // 2) * chunk

    def send_x(par, side, c):
        half, start = piece(c)
        part = (half, pl.ds(pl.multiple_of(PAD + start, 8), chunk))
        ours, theirs = ((1, last + 1), (last, 0))[side]
        return pltpu.make_async_remote_copy(
            src_ref=buffers[par].at[:, part[0], ours, part[1], :],
            dst_ref=buffers[par].at[:, part[0], theirs, part[1], :],
            send_sem=xs_sem.at[par],
            recv_sem=xr_sem.at[par, side, c],
            device_id={"tx": to_x[side]},
            device_id_type=MESH,
        )

    def send_z(par, side, group, first, count, halves=slice(None)):
        ours, theirs = ((PAD, PAD + depth), (PAD + depth - 1, PAD - 1))[side]
        return pltpu.make_async_remote_copy(
            src_ref=buffers[par].at[:, halves, pl.ds(first, count), pl.ds(ours, 1), :],
            dst_ref=buffers[par].at[:, halves, pl.ds(first, count), pl.ds(theirs, 1), :],
            send_sem=zs_sem.at[par],
            recv_sem=zr_sem.at[par, group],
            device_id={"dz": to_z[side]},
            device_id_type=MESH,
        )

    def when(condition, action):
        pl.when(condition)(action)

    def start_x(par, side, c, also=True):
        when(jnp.logical_and(has_x[side], also), lambda: send_x(par, side, c).start())

    def wait_for(sem, sides, one, two, also=True):
        both_sides = jnp.logical_and(sides[0], sides[1])
        when(jnp.logical_and(both_sides, also), lambda: pltpu.make_async_copy(two, two, sem).wait())
        when(jnp.logical_and(jnp.logical_not(both_sides), also), lambda: pltpu.make_async_copy(one, one, sem).wait())

    def sent_x(par, also=True):
        one, two = (buffers[par].at[:, :, pl.ds(1, n), pl.ds(PAD, depth), :] for n in (1, 2))
        wait_for(xs_sem.at[par], has_x, one, two, also)

    def start_z(par, side, group, also=True):
        def start():
            for first, count in GROUPS[group]:
                send_z(par, side, group, first, count).start()

        when(jnp.logical_and(has_z[side], also), start)

    def outer_rows(par, count, rows):
        return buffers[par].at[:, :, pl.ds(1, count), pl.ds(PAD, rows), :]

    def sent_z(par):
        wait_for(zs_sem.at[par], has_z, outer_rows(par, planes, 1), outer_rows(par, planes, 2))

    def arrived_z(par, group):
        count = sum(count for _, count in GROUPS[group])
        wait_for(zr_sem.at[par, group], has_z, outer_rows(par, count, 1), outer_rows(par, count, 2))

    def arrived_last_z(group):
        block = outer_rows(0, sum(count for _, count in GROUPS[group]), 1)
        when(has_z[1], lambda: pltpu.make_async_copy(block, block, zr_sem.at[0, group]).wait())

    def edge_group(side, half):
        return EDGES + 2 * side + half

    def start_edge_z(par, side, half, also=True):
        def start():
            for x in (1, last):
                send_z(par, side, edge_group(side, half), x, 1, half).start()

        when(jnp.logical_and(has_z[side], also), start)

    def arrived_edge_z(par, side, half, also=True):
        come = send_z(par, 1 - side, edge_group(1 - side, half), 1, 2, half)
        when(jnp.logical_and(has_z[side], also), come.wait_recv)

    def both(action, *args):
        for side in range(2):
            action(args[0], side, *args[1:])

    def start_first_z(side, group):
        row, theirs = ((0, PAD + depth), (depth - 1, PAD - 1))[side]

        def start():
            for first, count in GROUPS[group]:
                for f, r in fields:
                    for s in range(2):
                        pltpu.make_async_remote_copy(
                            src_ref=r.at[pl.ds(first - 1, count), pl.ds(row, 1), pl.ds(128 * s, 128)],
                            dst_ref=even.at[f, s, pl.ds(first, count), pl.ds(theirs, 1), :],
                            send_sem=zs_sem.at[0],
                            recv_sem=zr_sem.at[0, edge_group(side, s) if group == EDGES else group],
                            device_id={"dz": to_z[side]},
                            device_id_type=MESH,
                        ).start()

        when(has_z[side], start)

    def pass_word(hear, tell):
        for side in range(2):

            @pl.when(jnp.logical_and(has_z[side], hear))
            def _():
                pl.semaphore_wait(word_sem.at[side], 1)

        for side in range(2):

            @pl.when(jnp.logical_and(has_z[side], tell))
            def _():
                pl.semaphore_signal(
                    word_sem.at[1 - side], inc=1, device_id={"dz": to_z[side]}, device_id_type=MESH
                )

    pass_word(False, True)
    landed(0, even.at[:, :, pl.ds(1, 2), pl.ds(PAD, depth), :])
    for c in range(CHUNKS):
        both(start_x, 0, c)
        for side in range(2):
            for group in ((LOWER,), (EDGES,), (UPPER, LAST), (BESIDE,))[c]:
                start_first_z(side, group)
    landed(1, even.at[:, :, pl.ds(1, planes - 2), pl.ds(PAD, depth), :])
    landed(2, rate)

    def edge(step, new, c):
        old = 1 - new
        ahead = step < STEPS
        half, start = piece(c)
        below, above = c < CHUNKS // 2, c >= CHUNKS // 2
        arrived_edge_z(old, 0, half, below)
        arrived_edge_z(old, 1, half, above)
        sent_x(new, jnp.logical_and(c == 0, step >= 2))
        for side, x in ((0, 1), (1, last)):
            when(has_x[side], lambda: send_x(old, 1 - side, c).wait_recv())
            advance_half(buffers[old], buffers[new], rate, x, half, pl.multiple_of(start, chunk), chunk)
            start_x(new, side, c, ahead)
        start_edge_z(new, 0, half, below)
        start_edge_z(new, 1, half, jnp.logical_and(above, ahead))
        due = jnp.logical_and(c % 2 == 0, ahead)
        pass_word(due, jnp.logical_and(due, jnp.logical_or(step < STEPS - 1, c == 0)))

    def interior(new, low, high, stride=1):
        def plane(i, carry):
            advance(buffers[1 - new], buffers[new], rate, adjacent, low + i * stride, depth)
            return carry

        lax.fori_loop(0, (high - low + stride - 1) // stride, plane, 0)

    def ahead_of(step, new, c):
        old = 1 - new
        if not isinstance(c, int):
            pl.when(c == 2)(lambda: arrived_z(old, UPPER))
            interior(new, 4 * c + 1, 4 * c + 5)
            for at, group in ((1, LOWER), (2, UPPER)):
                start_z(new, 0, group, c == at)
                start_z(new, 1, group, jnp.logical_and(c == at, step + 1 < STEPS))

        elif c == 0:
            arrived_z(old, LOWER)
            sent_z(new)
            interior(new, 3, 5)
        else:
            arrived_z(old, LAST)
            interior(new, 13, 15)
            start_z(new, 0, LAST)
            start_z(new, 1, LAST, step + 1 < STEPS)

    def send_colors(peer, source, target, send_sem, recv_sem):
        return pltpu.make_async_remote_copy(
            src_ref=source(peer // (devices_z // 2)),
            dst_ref=target(dz),
            send_sem=send_sem,
            recv_sem=recv_sem,
            device_id={"dz": peer},
            device_id_type=MESH,
        )

    group = devices_z // 2
    far = [(1 - mine) * group + lax.rem(dz + by, group) for by in range(group)]
    near = [mine * group + lax.rem(dz + by, group) for by in range(1, group)]

    edge_halves, edge_peers = lambda half: edge_colors.at[0, half], lambda peers: all_edges.at[0, peers]
    inner_way = (lambda half: colors.at[half], lambda peers: all_colors.at[peers], cs_sem.at[0], cr_sem.at[0])
    edge_way = (edge_halves, edge_peers, es_sem.at[0], er_sem.at[0])
    pairs = pl.ds(1, len(PAIRS) - 1)
    pairs_way = (
        lambda half: edge_colors.at[pairs, half],
        lambda peers: all_edges.at[pairs, peers],
        es_sem.at[0],
        er_sem.at[0],
    )

    def render_pair(pair, side, half):
        x = jnp.where(side == 0, *PAIRS[pair])
        for ch, value in enumerate(march(even, x, half, depth, thickness)):
            edge_colors[pair, half, pl.ds(2 * ch + side, 1), :] = value

    def render(low, high, stride=1):
        def plane(i, carry):
            x = low + i * stride
            for s in range(2):
                for ch, value in enumerate(march(even, x, s, depth, thickness)):
                    colors[s, ch, pl.ds(x - 1, 1), :] = value
            return carry

        lax.fori_loop(0, (high - low + stride - 1) // stride, plane, 0)

    arrived_z(0, LOWER)
    interior(1, 3, 9)
    both(start_z, 1, LOWER)

    def pair(it, carry):
        for new in (1, 0):
            step = 2 * it + (1 if new else 2)
            final = step == STEPS
            ahead = step < STEPS
            old = 1 - new

            edge(step, new, 0)
            if new:

                @pl.when(it == 0)
                def _():
                    arrived_z(0, UPPER)
                    arrived_z(0, LAST)
                    interior(1, 9, 15)
                    both(start_z, 1, UPPER)
                    both(start_z, 1, LAST)

            arrived_z(old, BESIDE)
            interior(new, 2, 16, 13)
            start_z(new, 0, BESIDE)
            start_z(new, 1, BESIDE, ahead)
            if new:
                ahead_of(step, 0, 0)
            else:
                pl.when(ahead)(lambda: ahead_of(step, 1, 0))

                @pl.when(final)
                def _():
                    arrived_last_z(UPPER)
                    render(9, 13)
                    for peer in far + near:
                        send_colors(peer, *inner_way).start()
                    all_colors[dz] = colors[mine]

            def middle(c, carry, new=new, step=step, final=final, ahead=ahead):
                edge(step, new, c)
                if new:
                    ahead_of(step, 0, c)

                    @pl.when(jnp.logical_and(it == 1, c == 2))
                    def _():
                        arrived_last_z(LOWER)
                        render(3, 5)

                else:
                    pl.when(ahead)(lambda: ahead_of(step, 1, c))

                    @pl.when(jnp.logical_and(final, c == 1))
                    def _():
                        arrived_last_z(LAST)
                        arrived_last_z(BESIDE)

                        def sides(side, carry):
                            for pair in range(1, len(PAIRS)):
                                for half in range(2):
                                    render_pair(pair, side, half)
                            return carry

                        lax.fori_loop(0, 2, sides, 0)
                        for peer in far + near:
                            send_colors(peer, *pairs_way).start()
                        all_edges[pairs, dz] = edge_colors[pairs, mine]

                    @pl.when(jnp.logical_and(final, c == 2))
                    def _():
                        arrived_edge_z(0, 1, 1 - mine)
                        lax.fori_loop(0, 2, lambda side, _: render_pair(0, side, 1 - mine), None)
                        for peer in far:
                            send_colors(peer, *edge_way).start()

                return carry

            lax.fori_loop(1, 3, middle, 0)

            if new:
                edge(step, new, 3)
                ahead_of(step, 0, 3)
                pl.when(it == 1)(lambda: render(5, 9))
            else:

                @pl.when(ahead)
                def _():
                    edge(step, 0, 3)
                    ahead_of(step, 1, 3)

        return carry

    lax.fori_loop(0, STEPS // 2, pair, 0)

    arrived_edge_z(1, 1, mine)
    arrived_edge_z(0, 1, mine)
    later = jnp.where(lax.rem(tx, 4) == 0, 0, 1)

    def last_edge(k, carry):
        side = jnp.where(k == 0, 1 - later, later)
        x = jnp.where(side == 0, 1, last)
        block = odd.at[:, mine, x, pl.ds(PAD + depth - chunk, chunk), :]
        inward = pltpu.make_async_copy(block, block, xr_sem.at[1, 1 - side, CHUNKS - 1])
        when(jnp.where(side == 0, tx > 0, tx < devices_x - 1), lambda: inward.wait())
        advance_half(odd, even, rate, x, mine, depth - chunk, chunk)
        render_pair(0, side, mine)
        return carry

    lax.fori_loop(0, 2, last_edge, 0)
    for peer in near:
        send_colors(peer, *edge_way).start()
    all_edges[0, dz] = edge_colors[0, mine]

    sent_x(1)
    sent_z(1)
    block = outer_rows(0, planes, 1)
    when(has_z[0], lambda: pltpu.make_async_copy(block, block, zs_sem.at[0]).wait())
    peers = pl.ds(0, devices_z - 1)
    for ours, send_sem, recv_sem in ((all_colors.at[peers], cs_sem, cr_sem), (all_edges.at[:, peers], es_sem, er_sem)):
        for sem in (recv_sem, send_sem):
            pltpu.make_async_copy(ours, ours, sem.at[0]).wait()


def results(state, all_colors, all_edges, image_out, fuel_out, heat_out, image_ref, sem, image_sem):
    devices_z, _, planes, _ = all_colors.shape
    depth = fuel_out.shape[1]
    share = image_ref.shape[2]
    dz = lax.axis_index("dz")
    piece = planes // 4
    for first in range(0, planes, piece):
        for f, target in ((0, fuel_out), (1, heat_out)):
            for s in range(2):
                pltpu.make_async_copy(
                    state.at[f, s, pl.ds(1 + first, piece), pl.ds(PAD, depth), :],
                    target.at[pl.ds(first, piece), :, pl.ds(128 * s, 128)],
                    sem.at[f],
                ).start()
    shift = lax.rem(128 - share * lax.rem(dz, devices_z // 2), 128)
    image = compose([[all_colors[b, ch] for ch in range(4)] for b in range(devices_z)])
    for ch in range(4):
        image_ref[ch] = pltpu.roll(image[ch], shift, 1)[:, :share]
    for pair, planes_of in enumerate(PAIRS):
        rows = [[all_edges[pair, b, 2 * ch : 2 * ch + 2, :] for ch in range(4)] for b in range(devices_z)]
        image = compose(rows)
        for ch in range(4):
            value = pltpu.roll(image[ch], shift, 1)[:, :share]
            for side, x in enumerate(planes_of):
                image_ref[ch, x - 1 : x] = value[side : side + 1]
    shown = pltpu.make_async_copy(image_ref, image_out, image_sem)
    shown.start()
    shown.wait()
    for f, target in ((0, fuel_out), (1, heat_out)):
        pltpu.make_async_copy(target, target, sem.at[f]).wait()


def body(fuel, heat, rate):
    planes, depth, width = fuel.shape
    devices_x, devices_z = lax.axis_size("tx"), lax.axis_size("dz")
    sizes = (devices_x, devices_z, planes, depth, width)
    anywhere = pl.BlockSpec(memory_space=pltpu.HBM)
    local = pl.BlockSpec(memory_space=pltpu.VMEM)
    block = pltpu.VMEM((2, 2, planes + 2, depth + ROWS_AFTER, 128), jnp.float32)
    dma = pltpu.SemaphoreType.DMA
    arrived = pl.pallas_call(
        functools.partial(kernel, sizes),
        out_shape=(
            block,
            pltpu.VMEM((devices_z, 4, planes, 128), jnp.float32),
            pltpu.VMEM((len(PAIRS), devices_z, 8, 128), jnp.float32),
        ),
        in_specs=[anywhere] * 3,
        out_specs=(local,) * 3,
        scratch_shapes=[
            block,
            pltpu.VMEM((2, planes, depth, 128), jnp.float32),
            pltpu.VMEM((width, width), jnp.bfloat16),
            pltpu.VMEM((2, 4, planes, 128), jnp.float32),
            pltpu.VMEM((len(PAIRS), 2, 8, 128), jnp.float32),
            dma((3,)),
            dma((2,)),
            dma((2, 2, CHUNKS)),
            dma((2,)),
            dma((2, EDGES + 4)),
            dma((1,)),
            dma((1,)),
            dma((1,)),
            dma((1,)),
            pltpu.SemaphoreType.REGULAR((2,)),
        ],
        compiler_params=pltpu.CompilerParams(
            collective_id=0, has_side_effects=True, vmem_limit_bytes=40 * 2**20
        ),
    )(*(pltpu.with_memory_space_constraint(a, pltpu.HBM) for a in (fuel, heat, rate)))
    return pl.pallas_call(
        results,
        out_shape=(
            jax.ShapeDtypeStruct((4, planes, width // devices_z), jnp.float32),
            jax.ShapeDtypeStruct(fuel.shape, jnp.float32),
            jax.ShapeDtypeStruct(fuel.shape, jnp.float32),
        ),
        in_specs=[local] * 3,
        out_specs=(anywhere,) * 3,
        scratch_shapes=[
            pltpu.VMEM((4, planes, width // devices_z), jnp.float32),
            dma((2,)),
            dma,
        ],
        compiler_params=pltpu.CompilerParams(vmem_limit_bytes=40 * 2**20),
    )(*arrived)


def solution(mesh):
    placed = (P("tx", "dz", None),) * 3
    return jax.shard_map(
        body,
        mesh=mesh,
        in_specs=placed,
        out_specs=(P(None, "tx", "dz"), P("tx", "dz", None), P("tx", "dz", None)),
        check_vma=False,
    )
```

```python
import functools

import jax
import jax.numpy as jnp
from jax import lax
from jax.experimental import pallas as pl
from jax.experimental.pallas import tpu as pltpu
from jax.sharding import PartitionSpec as P

STEPS = 4
FUEL_SPREAD = 0.15
HEAT_SPREAD = 0.12
ACTIVATION = 1.5
RELEASE = 2.0
OPACITY = 1.5
LOG2E = 1.4426950408889634
MESH = pl.DeviceIdType.MESH

PAD = 8
ROWS_AFTER = 56
CHUNKS = 4
SEGMENTS = 8
GROUPS = (((2, 1), (15, 1)), ((3, 6),), ((9, 4),), ((13, 2),), ((1, 1), (16, 1)))
BESIDE, LOWER, UPPER, LAST, EDGES = range(5)
PAIRS = ((1, 16), (2, 15), (13, 14))


def split(value):
    high = value.astype(jnp.bfloat16)
    low = (value - high.astype(jnp.float32)).astype(jnp.bfloat16)
    return high, low


def step_of(src, dst, rate, x, start, rows, halves, center, across):
    here = pl.ds(start + PAD, rows)
    mixed = []
    for f, spread in ((0, FUEL_SPREAD), (1, HEAT_SPREAD)):
        row = []
        for k, s in enumerate(halves):
            view = src.at[f, s, x, pl.ds(start, rows + 2 * PAD), :]
            beside = view[PAD - 1 : PAD - 1 + rows] + view[PAD + 1 : PAD + 1 + rows]
            beside = beside + (src[f, s, x - 1, here, :] + src[f, s, x + 1, here, :])
            beside = beside + across[f][k]
            row.append((1.0 - 6.0 * spread) * center[f][k] + spread * beside)
        mixed.append(row)
    for k, s in enumerate(halves):
        fuel, heat = mixed[0][k], mixed[1][k]
        inverse = pl.reciprocal(1.0 + heat, approx=False)
        speed = jnp.exp2(ACTIVATION * LOG2E - (ACTIVATION * LOG2E) * inverse)
        burned = rate[s, x - 1, pl.ds(start, rows), :] * fuel * speed
        dst[0, s, x, here, :] = fuel - burned
        dst[1, s, x, here, :] = heat + RELEASE * burned


def advance(src, dst, rate, adjacent, x, rows):
    center = [[src[f, s, x, pl.ds(PAD, rows), :] for s in range(2)] for f in range(2)]
    parts = [split(jnp.concatenate(center[f], axis=1)) for f in range(2)]
    sums = jnp.dot(
        jnp.concatenate([*parts[0], *parts[1]], axis=0),
        adjacent[...],
        preferred_element_type=jnp.float32,
    )
    across = []
    for f in range(2):
        total = sums[2 * f * rows : (2 * f + 1) * rows] + sums[(2 * f + 1) * rows : (2 * f + 2) * rows]
        across.append((total[:, :128], total[:, 128:]))
    step_of(src, dst, rate, x, 0, rows, range(2), center, across)


def advance_half(src, dst, rate, x, s, start, rows):
    here = pl.ds(start + PAD, rows)
    center = [[src[f, s, x, here, :]] for f in range(2)]
    lane = lax.broadcasted_iota(jnp.int32, (rows, 128), 1)
    seam = jnp.where(s == 0, 127, 0)
    shift = jnp.where(s == 0, 127, 1)
    across = []
    for f in range(2):
        mine = center[f][0]
        total = jnp.where(lane == 0, 0.0, pltpu.roll(mine, 1, 1)) + jnp.where(lane == 127, 0.0, pltpu.roll(mine, 127, 1))
        other = pltpu.roll(src[f, 1 - s, x, here, :], shift, 1)
        across.append([total + jnp.where(lane == seam, other, 0.0)])
    step_of(src, dst, rate, x, start, rows, [s], center, across)


def march(state, x, s, depth, thickness):
    length = depth // SEGMENTS + 1
    full = depth - (SEGMENTS - 1) * length
    rate = -0.5 * thickness * LOG2E
    sub = lax.broadcasted_iota(jnp.int32, (SEGMENTS, 128), 0)
    zero = jnp.zeros((SEGMENTS, 128), jnp.float32)
    rows = lambda f, v: state[f, s, x, pl.ds(PAD + v, SEGMENTS, stride=length), :]
    red, green, blue, passed = zero, zero, zero, zero
    through = zero + 1.0
    fuel, heat = rows(0, 0), rows(1, 0)
    for v in range(length):
        next_fuel, next_heat = rows(0, v + 1), rows(1, v + 1)
        both_fuel, both_heat = fuel + next_fuel, heat + next_heat
        if v >= full:
            both_fuel = jnp.where(sub < SEGMENTS - 1, both_fuel, 0.0)
            both_heat = jnp.where(sub < SEGMENTS - 1, both_heat, 0.0)
        passed = passed + both_heat
        later = jnp.exp2(rate * passed)
        weight = through - later
        glow = 1.0 - 2.0 * pl.reciprocal(2.0 + both_heat, approx=False)
        shaded = weight * both_fuel
        red = red + weight * glow
        green = green + shaded
        blue = blue + shaded * glow
        through, fuel, heat = later, next_fuel, next_heat
    before = passed
    for by in (1, 2, 4):
        before = before + jnp.where(sub >= by, pltpu.roll(before, by, 0), 0.0)
    share = jnp.exp2(rate * (before - passed))
    return [
        jnp.sum(share * red, axis=0, keepdims=True),
        0.5 * jnp.sum(share * green, axis=0, keepdims=True),
        0.5 * jnp.sum(share * blue, axis=0, keepdims=True),
        (0.5 * thickness) * jnp.sum(passed, axis=0, keepdims=True),
    ]


def compose(pieces):
    before = jnp.zeros_like(pieces[0][3])
    total = [jnp.zeros_like(before) for _ in range(3)]
    for piece in pieces:
        share = jnp.exp2(-LOG2E * before)
        total = [t + share * c for t, c in zip(total, piece[:3])]
        before = before + piece[3]
    return total + [1.0 - jnp.exp2(-LOG2E * before)]


def kernel(
    sizes,
    fuel_ref,
    heat_ref,
    rate_ref,
    even,
    all_colors,
    all_edges,
    odd,
    rate,
    adjacent,
    colors,
    edge_colors,
    in_sem,
    xs_sem,
    xr_sem,
    zs_sem,
    zr_sem,
    cs_sem,
    cr_sem,
    es_sem,
    er_sem,
    word_sem,
):
    devices_x, devices_z, planes, depth, width = sizes
    tx, dz = lax.axis_index("tx"), lax.axis_index("dz")
    thickness = OPACITY / (depth * devices_z)
    buffers = (even, odd)
    chunk = 2 * depth // CHUNKS
    mine = dz // (devices_z // 2)
    last = planes
    has_x = (tx > 0, tx < devices_x - 1)
    has_z = (dz > 0, dz < devices_z - 1)
    to_x = (tx - 1, tx + 1)
    to_z = (dz - 1, dz + 1)

    barrier = pltpu.get_barrier_semaphore()
    for side in range(2):

        @pl.when(has_x[side])
        def _():
            pl.semaphore_signal(barrier, inc=1, device_id={"tx": to_x[side]}, device_id_type=MESH)

    for side in range(2):

        @pl.when(has_z[side])
        def _():
            pl.semaphore_signal(barrier, inc=1, device_id={"dz": to_z[side]}, device_id_type=MESH)

    def load(source, target, k, first, count, at, s):
        return pltpu.make_async_copy(
            source.at[pl.ds(first, count), :, pl.ds(128 * s, 128)], target.at[s, pl.ds(first + at, count)], in_sem.at[k]
        )

    even_rows = [even.at[f, :, :, pl.ds(PAD, depth), :] for f in range(2)]
    fields = ((0, fuel_ref), (1, heat_ref))
    edges = [load(r, even_rows[f], 0, x, 1, 1, s) for x in (0, planes - 1) for f, r in fields for s in range(2)]
    inner = [load(r, even_rows[f], 1, 1, planes - 2, 1, s) for f, r in fields for s in range(2)]
    rates = [load(rate_ref, rate, 2, 0, planes, 0, s) for s in range(2)]

    def landed(k, block):
        pltpu.make_async_copy(block, block, in_sem.at[k]).wait()

    for copy in edges + inner + rates:
        copy.start()

    for side, plane in ((0, 0), (1, last + 1)):

        @pl.when(jnp.logical_not(has_x[side]))
        def _():
            def clear(r, carry):
                for buffer in buffers:
                    for f in range(2):
                        for s in range(2):
                            rows = pl.ds(PAD + r * chunk, chunk)
                            buffer[f, s, plane, rows, :] = jnp.zeros((chunk, 128), jnp.float32)
                return carry

            lax.fori_loop(0, CHUNKS // 2, clear, 0)

    for side, at in ((0, 0), (1, PAD + depth)):

        @pl.when(jnp.logical_not(has_z[side]))
        def _():
            def clear(x, carry):
                for buffer in buffers:
                    for f in range(2):
                        for s in range(2):
                            buffer[f, s, x, at : at + PAD, :] = jnp.zeros((PAD, 128), jnp.float32)
                return carry

            lax.fori_loop(1, last + 1, clear, 0)

    i = lax.broadcasted_iota(jnp.int32, (width, width), 0)
    j = lax.broadcasted_iota(jnp.int32, (width, width), 1)
    adjacent[...] = jnp.where(jnp.abs(i - j) == 1, 1.0, 0.0).astype(jnp.bfloat16)

    greeted = sum(jnp.where(near, 1, 0) for near in has_x + has_z)
    pl.semaphore_wait(barrier, greeted)

    def piece(c):
        return jnp.where(c % 2 == 0, 1 - mine, mine), (c // 2) * chunk

    def send_x(par, side, c):
        half, start = piece(c)
        part = (half, pl.ds(pl.multiple_of(PAD + start, 8), chunk))
        ours, theirs = ((1, last + 1), (last, 0))[side]
        return pltpu.make_async_remote_copy(
            src_ref=buffers[par].at[:, part[0], ours, part[1], :],
            dst_ref=buffers[par].at[:, part[0], theirs, part[1], :],
            send_sem=xs_sem.at[par],
            recv_sem=xr_sem.at[par, side, c],
            device_id={"tx": to_x[side]},
            device_id_type=MESH,
        )

    def send_z(par, side, group, first, count, halves=slice(None)):
        ours, theirs = ((PAD, PAD + depth), (PAD + depth - 1, PAD - 1))[side]
        return pltpu.make_async_remote_copy(
            src_ref=buffers[par].at[:, halves, pl.ds(first, count), pl.ds(ours, 1), :],
            dst_ref=buffers[par].at[:, halves, pl.ds(first, count), pl.ds(theirs, 1), :],
            send_sem=zs_sem.at[par],
            recv_sem=zr_sem.at[par, group],
            device_id={"dz": to_z[side]},
            device_id_type=MESH,
        )

    def when(condition, action):
        pl.when(condition)(action)

    def start_x(par, side, c, also=True):
        when(jnp.logical_and(has_x[side], also), lambda: send_x(par, side, c).start())

    def wait_for(sem, sides, one, two, also=True):
        both_sides = jnp.logical_and(sides[0], sides[1])
        when(jnp.logical_and(both_sides, also), lambda: pltpu.make_async_copy(two, two, sem).wait())
        when(jnp.logical_and(jnp.logical_not(both_sides), also), lambda: pltpu.make_async_copy(one, one, sem).wait())

    def sent_x(par, also=True):
        one, two = (buffers[par].at[:, :, pl.ds(1, n), pl.ds(PAD, depth), :] for n in (1, 2))
        wait_for(xs_sem.at[par], has_x, one, two, also)

    def start_z(par, side, group, also=True):
        def start():
            for first, count in GROUPS[group]:
                send_z(par, side, group, first, count).start()

        when(jnp.logical_and(has_z[side], also), start)

    def outer_rows(par, count, rows):
        return buffers[par].at[:, :, pl.ds(1, count), pl.ds(PAD, rows), :]

    def sent_z(par):
        wait_for(zs_sem.at[par], has_z, outer_rows(par, planes, 1), outer_rows(par, planes, 2))

    def arrived_z(par, group):
        count = sum(count for _, count in GROUPS[group])
        wait_for(zr_sem.at[par, group], has_z, outer_rows(par, count, 1), outer_rows(par, count, 2))

    def arrived_last_z(group):
        block = outer_rows(0, sum(count for _, count in GROUPS[group]), 1)
        when(has_z[1], lambda: pltpu.make_async_copy(block, block, zr_sem.at[0, group]).wait())

    def edge_group(side, half):
        return EDGES + 2 * side + half

    def start_edge_z(par, side, half, also=True):
        def start():
            for x in (1, last):
                send_z(par, side, edge_group(side, half), x, 1, half).start()

        when(jnp.logical_and(has_z[side], also), start)

    def arrived_edge_z(par, side, half, also=True):
        come = send_z(par, 1 - side, edge_group(1 - side, half), 1, 2, half)
        when(jnp.logical_and(has_z[side], also), come.wait_recv)

    def both(action, *args):
        for side in range(2):
            action(args[0], side, *args[1:])

    def start_first_z(side, group):
        row, theirs = ((0, PAD + depth), (depth - 1, PAD - 1))[side]

        def start():
            for first, count in GROUPS[group]:
                for f, r in fields:
                    for s in range(2):
                        pltpu.make_async_remote_copy(
                            src_ref=r.at[pl.ds(first - 1, count), pl.ds(row, 1), pl.ds(128 * s, 128)],
                            dst_ref=even.at[f, s, pl.ds(first, count), pl.ds(theirs, 1), :],
                            send_sem=zs_sem.at[0],
                            recv_sem=zr_sem.at[0, edge_group(side, s) if group == EDGES else group],
                            device_id={"dz": to_z[side]},
                            device_id_type=MESH,
                        ).start()

        when(has_z[side], start)

    def pass_word(hear, tell):
        for side in range(2):

            @pl.when(jnp.logical_and(has_z[side], hear))
            def _():
                pl.semaphore_wait(word_sem.at[side], 1)

        for side in range(2):

            @pl.when(jnp.logical_and(has_z[side], tell))
            def _():
                pl.semaphore_signal(
                    word_sem.at[1 - side], inc=1, device_id={"dz": to_z[side]}, device_id_type=MESH
                )

    pass_word(False, True)
    landed(0, even.at[:, :, pl.ds(1, 2), pl.ds(PAD, depth), :])
    for c in range(CHUNKS):
        both(start_x, 0, c)
        for side in range(2):
            for group in ((LOWER,), (EDGES,), (UPPER, LAST), (BESIDE,))[c]:
                start_first_z(side, group)
    landed(1, even.at[:, :, pl.ds(1, planes - 2), pl.ds(PAD, depth), :])
    landed(2, rate)

    def edge(step, new, c):
        old = 1 - new
        ahead = step < STEPS
        half, start = piece(c)
        below, above = c < CHUNKS // 2, c >= CHUNKS // 2
        arrived_edge_z(old, 0, half, below)
        arrived_edge_z(old, 1, half, above)
        sent_x(new, jnp.logical_and(c == 0, step >= 2))
        for side, x in ((0, 1), (1, last)):
            when(has_x[side], lambda: send_x(old, 1 - side, c).wait_recv())
            advance_half(buffers[old], buffers[new], rate, x, half, pl.multiple_of(start, chunk), chunk)
            start_x(new, side, c, ahead)
        start_edge_z(new, 0, half, below)
        start_edge_z(new, 1, half, jnp.logical_and(above, ahead))
        due = jnp.logical_and(c % 2 == 0, ahead)
        pass_word(due, jnp.logical_and(due, jnp.logical_or(step < STEPS - 1, c == 0)))

    def interior(new, low, high, stride=1):
        def plane(i, carry):
            advance(buffers[1 - new], buffers[new], rate, adjacent, low + i * stride, depth)
            return carry

        lax.fori_loop(0, (high - low + stride - 1) // stride, plane, 0)

    def ahead_of(step, new, c):
        old = 1 - new
        if not isinstance(c, int):
            pl.when(c == 2)(lambda: arrived_z(old, UPPER))
            interior(new, 4 * c + 1, 4 * c + 5)
            for at, group in ((1, LOWER), (2, UPPER)):
                start_z(new, 0, group, c == at)
                start_z(new, 1, group, jnp.logical_and(c == at, step + 1 < STEPS))

        elif c == 0:
            arrived_z(old, LOWER)
            sent_z(new)
            interior(new, 3, 5)
        else:
            arrived_z(old, LAST)
            interior(new, 13, 15)
            start_z(new, 0, LAST)
            start_z(new, 1, LAST, step + 1 < STEPS)
            arrived_z(old, BESIDE)
            interior(new, 2, 16, 13)
            start_z(new, 0, BESIDE)
            start_z(new, 1, BESIDE, step + 1 < STEPS)

    def send_colors(peer, source, target, send_sem, recv_sem):
        return pltpu.make_async_remote_copy(
            src_ref=source(peer // (devices_z // 2)),
            dst_ref=target(dz),
            send_sem=send_sem,
            recv_sem=recv_sem,
            device_id={"dz": peer},
            device_id_type=MESH,
        )

    group = devices_z // 2
    far = [(1 - mine) * group + lax.rem(dz + by, group) for by in range(group)]
    near = [mine * group + lax.rem(dz + by, group) for by in (2, 1, 3)]

    edge_halves, edge_peers = lambda half: edge_colors.at[0, half], lambda peers: all_edges.at[0, peers]
    inner_way = (lambda half: colors.at[half], lambda peers: all_colors.at[peers], cs_sem.at[0], cr_sem.at[0])
    edge_way = (edge_halves, edge_peers, es_sem.at[0], er_sem.at[0])
    pairs = pl.ds(1, len(PAIRS) - 1)
    pairs_way = (
        lambda half: edge_colors.at[pairs, half],
        lambda peers: all_edges.at[pairs, peers],
        es_sem.at[0],
        er_sem.at[0],
    )

    def render_pair(pair, side, half):
        x = jnp.where(side == 0, *PAIRS[pair])
        for ch, value in enumerate(march(even, x, half, depth, thickness)):
            edge_colors[pair, half, pl.ds(2 * ch + side, 1), :] = value

    def render(low, high, stride=1):
        def plane(i, carry):
            x = low + i * stride
            for s in range(2):
                for ch, value in enumerate(march(even, x, s, depth, thickness)):
                    colors[s, ch, pl.ds(x - 1, 1), :] = value
            return carry

        lax.fori_loop(0, (high - low + stride - 1) // stride, plane, 0)

    arrived_z(0, LOWER)
    interior(1, 3, 9)
    both(start_z, 1, LOWER)

    def pair(it, carry):
        for new in (1, 0):
            step = 2 * it + (1 if new else 2)
            final = step == STEPS
            ahead = step < STEPS
            old = 1 - new

            edge(step, new, 0)
            if new:

                @pl.when(it == 0)
                def _():
                    arrived_z(0, UPPER)
                    arrived_z(0, LAST)
                    interior(1, 9, 15)
                    both(start_z, 1, UPPER)
                    both(start_z, 1, LAST)
                    arrived_z(0, BESIDE)
                    interior(1, 2, 16, 13)
                    both(start_z, 1, BESIDE)

            if new:
                ahead_of(step, 0, 0)
            else:
                pl.when(ahead)(lambda: ahead_of(step, 1, 0))

                @pl.when(final)
                def _():
                    arrived_last_z(UPPER)
                    render(5, 13)
                    for peer in far + near:
                        send_colors(peer, *inner_way).start()
                    all_colors[dz] = colors[mine]

            def middle(c, carry, new=new, step=step, final=final, ahead=ahead):
                edge(step, new, c)
                if new:
                    ahead_of(step, 0, c)

                    @pl.when(jnp.logical_and(it == 1, c == 2))
                    def _():
                        arrived_last_z(LOWER)
                        render(3, 5)

                else:
                    pl.when(ahead)(lambda: ahead_of(step, 1, c))

                    @pl.when(jnp.logical_and(final, c == 1))
                    def _():
                        arrived_last_z(LAST)
                        arrived_last_z(BESIDE)

                        def sides(side, carry):
                            for pair in range(1, len(PAIRS)):
                                for half in range(2):
                                    render_pair(pair, side, half)
                            return carry

                        lax.fori_loop(0, 2, sides, 0)
                        for peer in far + near:
                            send_colors(peer, *pairs_way).start()
                        all_edges[pairs, dz] = edge_colors[pairs, mine]

                    @pl.when(jnp.logical_and(final, c == 2))
                    def _():
                        arrived_edge_z(0, 1, 1 - mine)
                        lax.fori_loop(0, 2, lambda side, _: render_pair(0, side, 1 - mine), None)
                        for peer in far:
                            send_colors(peer, *edge_way).start()

                return carry

            lax.fori_loop(1, 3, middle, 0)

            if new:
                edge(step, new, 3)
                ahead_of(step, 0, 3)
            else:

                @pl.when(ahead)
                def _():
                    edge(step, 0, 3)
                    ahead_of(step, 1, 3)

        return carry

    lax.fori_loop(0, STEPS // 2, pair, 0)

    arrived_edge_z(1, 1, mine)
    later = jnp.where(lax.rem(tx, 4) == 0, 0, 1)

    def last_edge(k, carry):
        side = jnp.where(k == 0, 1 - later, later)
        x = jnp.where(side == 0, 1, last)
        block = odd.at[:, mine, x, pl.ds(PAD + depth - chunk, chunk), :]
        inward = pltpu.make_async_copy(block, block, xr_sem.at[1, 1 - side, CHUNKS - 1])
        when(jnp.where(side == 0, tx > 0, tx < devices_x - 1), lambda: inward.wait())
        advance_half(odd, even, rate, x, mine, depth - chunk, chunk)
        arrived_edge_z(0, 1, mine, k == 0)
        render_pair(0, side, mine)
        return carry

    lax.fori_loop(0, 2, last_edge, 0)
    for peer in near:
        send_colors(peer, *edge_way).start()
    all_edges[0, dz] = edge_colors[0, mine]

    sent_x(1)
    sent_z(1)
    block = outer_rows(0, planes, 1)
    when(has_z[0], lambda: pltpu.make_async_copy(block, block, zs_sem.at[0]).wait())
    peers = pl.ds(0, devices_z - 1)
    for ours, send_sem, recv_sem in ((all_colors.at[peers], cs_sem, cr_sem), (all_edges.at[:, peers], es_sem, er_sem)):
        for sem in (recv_sem, send_sem):
            pltpu.make_async_copy(ours, ours, sem.at[0]).wait()


def results(state, all_colors, all_edges, image_out, fuel_out, heat_out, image_ref, sem, image_sem):
    devices_z, _, planes, _ = all_colors.shape
    depth = fuel_out.shape[1]
    share = image_ref.shape[2]
    dz = lax.axis_index("dz")
    piece = planes // 4
    for first in range(0, planes, piece):
        for f, target in ((0, fuel_out), (1, heat_out)):
            for s in range(2):
                pltpu.make_async_copy(
                    state.at[f, s, pl.ds(1 + first, piece), pl.ds(PAD, depth), :],
                    target.at[pl.ds(first, piece), :, pl.ds(128 * s, 128)],
                    sem.at[f],
                ).start()
    shift = lax.rem(128 - share * lax.rem(dz, devices_z // 2), 128)
    image = compose([[all_colors[b, ch] for ch in range(4)] for b in range(devices_z)])
    for ch in range(4):
        image_ref[ch] = pltpu.roll(image[ch], shift, 1)[:, :share]
    for pair, planes_of in enumerate(PAIRS):
        rows = [[all_edges[pair, b, 2 * ch : 2 * ch + 2, :] for ch in range(4)] for b in range(devices_z)]
        image = compose(rows)
        for ch in range(4):
            value = pltpu.roll(image[ch], shift, 1)[:, :share]
            for side, x in enumerate(planes_of):
                image_ref[ch, x - 1 : x] = value[side : side + 1]
    shown = pltpu.make_async_copy(image_ref, image_out, image_sem)
    shown.start()
    shown.wait()
    for f, target in ((0, fuel_out), (1, heat_out)):
        pltpu.make_async_copy(target, target, sem.at[f]).wait()


def body(fuel, heat, rate):
    planes, depth, width = fuel.shape
    devices_x, devices_z = lax.axis_size("tx"), lax.axis_size("dz")
    sizes = (devices_x, devices_z, planes, depth, width)
    anywhere = pl.BlockSpec(memory_space=pltpu.HBM)
    local = pl.BlockSpec(memory_space=pltpu.VMEM)
    block = pltpu.VMEM((2, 2, planes + 2, depth + ROWS_AFTER, 128), jnp.float32)
    dma = pltpu.SemaphoreType.DMA
    arrived = pl.pallas_call(
        functools.partial(kernel, sizes),
        out_shape=(
            block,
            pltpu.VMEM((devices_z, 4, planes, 128), jnp.float32),
            pltpu.VMEM((len(PAIRS), devices_z, 8, 128), jnp.float32),
        ),
        in_specs=[anywhere] * 3,
        out_specs=(local,) * 3,
        scratch_shapes=[
            block,
            pltpu.VMEM((2, planes, depth, 128), jnp.float32),
            pltpu.VMEM((width, width), jnp.bfloat16),
            pltpu.VMEM((2, 4, planes, 128), jnp.float32),
            pltpu.VMEM((len(PAIRS), 2, 8, 128), jnp.float32),
            dma((3,)),
            dma((2,)),
            dma((2, 2, CHUNKS)),
            dma((2,)),
            dma((2, EDGES + 4)),
            dma((1,)),
            dma((1,)),
            dma((1,)),
            dma((1,)),
            pltpu.SemaphoreType.REGULAR((2,)),
        ],
        compiler_params=pltpu.CompilerParams(
            collective_id=0, has_side_effects=True, vmem_limit_bytes=40 * 2**20
        ),
    )(*(pltpu.with_memory_space_constraint(a, pltpu.HBM) for a in (fuel, heat, rate)))
    return pl.pallas_call(
        results,
        out_shape=(
            jax.ShapeDtypeStruct((4, planes, width // devices_z), jnp.float32),
            jax.ShapeDtypeStruct(fuel.shape, jnp.float32),
            jax.ShapeDtypeStruct(fuel.shape, jnp.float32),
        ),
        in_specs=[local] * 3,
        out_specs=(anywhere,) * 3,
        scratch_shapes=[
            pltpu.VMEM((4, planes, width // devices_z), jnp.float32),
            dma((2,)),
            dma,
        ],
        compiler_params=pltpu.CompilerParams(vmem_limit_bytes=40 * 2**20),
    )(*arrived)


def solution(mesh):
    placed = (P("tx", "dz", None),) * 3
    return jax.shard_map(
        body,
        mesh=mesh,
        in_specs=placed,
        out_specs=(P(None, "tx", "dz"), P("tx", "dz", None), P("tx", "dz", None)),
        check_vma=False,
    )
```
